128 devices in a mesh: section: 2 (over y_hi), ep: 32 (over x, z, core), tp: 2 (over y_lo).
Axes of the slice: x: 4, y: 4 (y_hi: 2, y_lo: 2; y = y_hi * 2 + y_lo), z: 4, core: 2. Of those that a mesh axis runs over, the one named last changes fastest.
Arguments:
- x_in: bfloat16 [2, 2048, 1536], P(None, 'ep'), may hold values from -6 to 6
- cotangent: bfloat16 [2, 2048, 1536], P(None, ('ep', 'tp')), may hold values from -6 to 6
- norm1_gain: float32 [2, 1536], P('section'), may hold values from 0.5 to 1.5
- wq: bfloat16 [2, 1536, 1536], P('section', None, 'tp'), may hold values from -0.15625 to 0.15625
- wk: bfloat16 [2, 1536, 512], P('section', None, 'tp'), may hold values from -0.15625 to 0.15625
- wv: bfloat16 [2, 1536, 512], P('section', None, 'tp'), may hold values from -0.15625 to 0.15625
- wo: bfloat16 [2, 1536, 1536], P('section', 'tp'), may hold values from -4 to 4
- norm2_gain: float32 [2, 1536], P('section'), may hold values from 0.5 to 1.5
- router: bfloat16 [2, 1536, 40], P('section'), may hold values from -0.078125 to 0.078125
- w_gate: bfloat16 [2, 1536, 20480], P('section', None, 'ep'), may hold values from -0.15625 to 0.15625
- w_up: bfloat16 [2, 1536, 20480], P('section', None, 'ep'), may hold values from -0.15625 to 0.15625
- w_down: bfloat16 [2, 20480, 1536], P('section', 'ep'), may hold values from -1.5 to 1.5
- routes: int32 [2, 2, 2048, 8], P('section', None, 'ep'), may hold values from 0 to 39, all different within a row; in each aligned block of 32 rows (0 to 31, 32 to 63, ..., all dimensions but the last counted through in order) at most 8 rows name the same one
Outputs:
- activations: bfloat16 [2, 2, 2048, 1536], P('section', None, 'ep')
- input_grads: bfloat16 [2, 2, 2048, 1536], P('section', None, ('ep', 'tp'))
- grad_norm1: float32 [2, 1536], P('section')
- grad_wq: float32 [2, 1536, 1536], P('section', None, 'tp')
- grad_wk: float32 [2, 1536, 512], P('section', None, 'tp')
- grad_wv: float32 [2, 1536, 512], P('section', None, 'tp')
- grad_wo: float32 [2, 1536, 1536], P('section', 'tp')
- grad_norm2: float32 [2, 1536], P('section')
- grad_router: float32 [2, 1536, 40], P('section')
- grad_gate: float32 [2, 1536, 20480], P('section', None, 'ep')
- grad_up: float32 [2, 1536, 20480], P('section', None, 'ep')
- grad_down: float32 [2, 20480, 1536], P('section', 'ep')
The draws below stay inside these ranges and needn't reach their ends.
Inputs may be any that keep to these rules, and one draw needn't show every extreme that they name: `routes`: each row names 8 different experts; in each aligned block of 32 rows (all leading dimensions taken together) no expert is named more than 8 times, a bound that some block reaches.
All inputs are finite; a program needn't handle non-finite values.
Results may differ from the reference program's by a relative error of at most 0.033.
Values may be sent and summed in bfloat16 or wider, within the bound.
No kernel may reach another device: no remote copies, remote signals or barrier semaphores. Data moves between devices by JAX's collectives and lax.ppermute only.
A program may use at most 256 MiB of HBM per device.

```python
import math
import jax
import jax.numpy as jnp
import numpy as np
from jax import lax

MODEL_DIM = 1536
QUERY_HEADS = 24
KEY_VALUE_HEADS = 8
HEAD_SIZE = 64
EXPERTS = 40
EFF = 512
TOPK = 8
BLOCK = 128
MICRO = 2
SEQ_DEV = 64
CAP = 8
LENGTH = 2048
N_SECTION = 2
N_TP = 2


def block_scale(rng, extent, shards, smallest, largest):
    loudness = 1.0
    for position, blocks in shards:
        draws = jax.random.uniform(jax.random.fold_in(jax.random.fold_in(rng, 6), position), (blocks,), jnp.float32, smallest / len(shards), largest / len(shards))
        loudness = loudness * jnp.repeat(jnp.exp(draws), extent[position] // blocks).reshape((-1,) + (1,) * (len(extent) - 1 - position))
    return loudness


def deal_out(own_key, own, number, rows, count, top, bound, skew):
    ranking = jax.random.permutation(own_key, count)
    packed, usual = load_shares(count, rows * top, bound, skew, True), load_shares(count, rows * top, bound, skew, False)
    places = jnp.arange(count)

    def named(sizes, offset_by):
        used = int((sizes > 0).sum())
        fixed = max(1, used // 4)
        passed = fixed + (places - fixed + offset_by * (used - fixed)) % max(1, count - fixed)
        return jnp.zeros((count,), jnp.int32).at[ranking[jnp.where(places < fixed, places, passed)]].set(jnp.asarray(sizes, jnp.int32))

    sizes = jnp.where(number % 4 == 0, named(packed, number // 4), named(usual, number - number // 4 - 1))
    mixed = jax.random.permutation(jax.random.fold_in(own, 3), count)
    donor, receiver = mixed[0:count // 2 * 2:2], mixed[1:count // 2 * 2:2]
    slack = jnp.minimum(sizes[donor] - 1, bound - sizes[receiver]) // 2
    slack = jnp.where((donor == ranking[0]) | (receiver == ranking[0]) | (sizes[receiver] == 0), 0, jnp.maximum(slack, 0))
    passed = jax.random.randint(jax.random.fold_in(own, 4), (count // 2,), 0, 1 << 20) % (slack + 1)
    sizes = sizes.at[donor].add(-passed).at[receiver].add(passed)
    items = jnp.searchsorted(jnp.cumsum(sizes), jnp.arange(rows * top), side="right").astype(jnp.int32)
    listing = items.reshape(top, rows).T
    listing = listing[jax.random.permutation(jax.random.fold_in(own, 1), rows)]
    offset_by = jax.random.randint(jax.random.fold_in(own, 2), (rows, 1), 0, top)
    return jnp.take_along_axis(listing, (jnp.arange(top)[None, :] + offset_by) % top, axis=1)


def load_shares(count, total, most, lean, full):
    portions = [(1 << 20) // math.isqrt(rank ** lean) + 1 for rank in range(1, count + 1)]
    largest = most if full else min(most, max(-(-total // count), total * portions[0] // sum(portions)))
    least = 1 if total - largest >= count - 1 else 0
    given, spare = [largest] + [least] * (count - 1), total - largest - least * (count - 1)
    while spare > 0:
        movable = [i for i in range(1, count) if given[i] < largest] or [i for i in range(1, count) if given[i] < most]
        whole, budget = sum([portions[i] for i in movable]), spare
        for i in movable:
            extra = min(most - given[i], max(1, budget * portions[i] // whole), spare)
            given[i] = given[i] + extra
            spare = spare - extra
    return np.array(given)


def normal_values(key, extent, width, bound, cuts=(), kind=jnp.bfloat16):
    level = block_scale(key, extent, cuts, -0.22, 0.18) if cuts else 1.0
    array = jax.random.normal(key, extent, jnp.float32) * width * level
    return jnp.minimum(jnp.maximum(array, -bound), bound).astype(kind)


def setup_inputs(seed: int = 0) -> dict:
    arg_keys = jax.random.split(jax.random.key(seed), 14)
    x_in = normal_values(arg_keys[0], (MICRO, LENGTH, MODEL_DIM), 1.0, 6.0, ((1, 32),))
    cotangent = normal_values(arg_keys[1], (MICRO, LENGTH, MODEL_DIM), 1.0, 6.0, ((1, 64),))
    norm1_gain = jnp.clip(1.0 + 0.1 * jax.random.normal(arg_keys[2], (N_SECTION, MODEL_DIM), jnp.float32), 0.5, 1.5)
    wq = normal_values(arg_keys[3], (N_SECTION, MODEL_DIM, QUERY_HEADS * HEAD_SIZE), MODEL_DIM ** -0.5, 0.15625, ((0, 2), (2, 2)))
    wk = normal_values(arg_keys[4], (N_SECTION, MODEL_DIM, KEY_VALUE_HEADS * HEAD_SIZE), MODEL_DIM ** -0.5, 0.15625, ((0, 2), (2, 2)))
    wv = normal_values(arg_keys[5], (N_SECTION, MODEL_DIM, KEY_VALUE_HEADS * HEAD_SIZE), MODEL_DIM ** -0.5, 0.15625, ((0, 2), (2, 2)))
    wo = normal_values(arg_keys[6], (N_SECTION, QUERY_HEADS * HEAD_SIZE, MODEL_DIM), 2 ** -0.5, 4.0, ((0, 2), (1, 2)))
    norm2_gain = jnp.clip(1.0 + 0.1 * jax.random.normal(arg_keys[7], (N_SECTION, MODEL_DIM), jnp.float32), 0.5, 1.5)
    router = normal_values(arg_keys[8], (N_SECTION, MODEL_DIM, EXPERTS), (0.5 * MODEL_DIM ** -0.5), 0.078125, ((0, 2),))
    w_gate = normal_values(arg_keys[9], (N_SECTION, MODEL_DIM, EXPERTS * EFF), MODEL_DIM ** -0.5, 0.15625, ((0, 2), (2, 32)))
    w_up = normal_values(arg_keys[10], (N_SECTION, MODEL_DIM, EXPERTS * EFF), MODEL_DIM ** -0.5, 0.15625, ((0, 2), (2, 32)))
    w_down = normal_values(arg_keys[11], (N_SECTION, EXPERTS * EFF, MODEL_DIM), (EFF // 32) ** -0.5, 1.5, ((0, 2), (1, 32)))
    routes_keys = jax.random.split(jax.random.fold_in(arg_keys[12], 1), N_SECTION * MICRO * LENGTH // (SEQ_DEV // N_TP))
    routes_turns = jax.random.permutation(jax.random.fold_in(arg_keys[12], 3), N_SECTION * MICRO * LENGTH // (SEQ_DEV // N_TP))
    routes = jax.vmap(lambda own, number: deal_out(jax.random.fold_in(arg_keys[12], 2), own, number, SEQ_DEV // N_TP, EXPERTS, TOPK, CAP, 0))(routes_keys, routes_turns).reshape((N_SECTION, MICRO, LENGTH, TOPK))
    return dict(x_in=x_in, cotangent=cotangent, norm1_gain=norm1_gain, wq=wq, wk=wk, wv=wv, wo=wo, norm2_gain=norm2_gain, router=router, w_gate=w_gate, w_up=w_up, w_down=w_down, routes=routes)


@jax.custom_vjp
def lower_precision(v):
    return lax.optimization_barrier(v.astype(jnp.bfloat16)).astype(jnp.float32)

@jax.custom_vjp
def lower_backward(v):
    return v

def low_keep(v):
    return (lower_precision(v), None)

def low_pass(kept, grad):
    return (grad,)

def back_keep(v):
    return (v, None)

def back_low(kept, grad):
    return (lower_precision(grad),)
lower_precision.defvjp(low_keep, low_pass)
lower_backward.defvjp(back_keep, back_low)
epsilon = 1e-05
highest_precision = lax.Precision.HIGHEST

def inverse_root(values):
    return lax.rsqrt(lax.optimization_barrier(jnp.mean(values * values, axis=-1, keepdims=True)) + epsilon)

def apply_rotation(values, cosine_table, sine_values):
    half_dim = values.shape[-1] // 2
    first_half = values[..., :half_dim]
    second_half = values[..., half_dim:]
    cos_wide = cosine_table[:, None, :]
    sin_wide = sine_values[:, None, :]
    return jnp.concatenate([first_half * cos_wide - second_half * sin_wide, second_half * cos_wide + first_half * sin_wide], axis=-1)

def angles(sequence_length):
    half_dim = HEAD_SIZE // 2
    frequency = 10000.0 ** (-jnp.arange(half_dim, dtype=jnp.float32) * 2.0 / HEAD_SIZE)
    phase_grid = jnp.arange(sequence_length, dtype=jnp.float32)[:, None] * frequency[None, :]
    return (jnp.cos(phase_grid), jnp.sin(phase_grid))

def attend(queries, keys, values):
    sequence_length = queries.shape[0]
    query_block = min(512, sequence_length)
    block_count = sequence_length // query_block
    key_positions = jnp.arange(sequence_length, dtype=jnp.int32)

    def score_block(block_index):
        block_start = (block_index * query_block).astype(jnp.int32)
        query_part = lax.dynamic_slice_in_dim(queries, block_start, query_block, 0)
        scores = lower_backward(jnp.einsum('qgjd,kgd->gjqk', query_part, keys, precision=highest_precision) * 0.125)
        row_ids = block_start + jnp.arange(query_block, dtype=jnp.int32)
        allowed = row_ids[:, None] >= key_positions[None, :]
        scores = jnp.where(allowed, scores, -1e+30)
        probabilities = lower_precision(jax.nn.softmax(scores, axis=-1))
        return jnp.einsum('gjqk,kgd->qgjd', probabilities, values, precision=highest_precision)
    results = lax.map(jax.checkpoint(score_block), jnp.arange(block_count, dtype=jnp.int32))
    return results.reshape(sequence_length, -1)

def slots_of(route_rows):
    expert_hits = (route_rows[:, :, None] == jnp.arange(EXPERTS, dtype=jnp.int32)[None, None, :]).astype(jnp.int32)
    per_row = lax.optimization_barrier(jnp.sum(expert_hits, axis=1))
    before = jnp.cumsum(per_row, axis=0) - per_row
    return lax.optimization_barrier(jnp.sum(expert_hits * before[:, None, :], axis=-1))

def experts_apply(rows_all, gate_all, up_all, down_all):

    def one_expert(operands):
        block_rows, gate_mat, up_mat, down_mat = operands
        gate_pre = lower_backward(jnp.dot(block_rows, gate_mat, precision=highest_precision))
        up_pre = lower_backward(jnp.dot(block_rows, up_mat, precision=highest_precision))
        hidden = lower_precision(jax.nn.silu(gate_pre) * up_pre)
        block_count = EFF // BLOCK
        pieces = jnp.einsum('mbh,bhd->mbd', hidden.reshape(-1, block_count, BLOCK), down_mat.reshape(block_count, BLOCK, MODEL_DIM), precision=highest_precision)
        return lax.optimization_barrier(jnp.sum(lower_precision(lower_backward(pieces)), axis=1))
    return lax.map(jax.checkpoint(one_expert), (rows_all, gate_all, up_all, down_all))

def layer_forward(inputs, gain_one, query_w, key_weight, value_weight, output_w, gain_two, router_w, gate_w, up_w, down_w, route_ids):
    sequence_length = inputs.shape[0]
    cosine_table, sine_values = angles(sequence_length)
    normalized_rows = lower_precision(inputs * inverse_root(inputs) * gain_one)
    query_projected = lower_backward(jnp.dot(normalized_rows, query_w, precision=highest_precision)).reshape(sequence_length, QUERY_HEADS, HEAD_SIZE)
    key_projected = lower_backward(jnp.dot(normalized_rows, key_weight, precision=highest_precision)).reshape(sequence_length, KEY_VALUE_HEADS, HEAD_SIZE)
    value_projected = lower_precision(lower_backward(jnp.dot(normalized_rows, value_weight, precision=highest_precision))).reshape(sequence_length, KEY_VALUE_HEADS, HEAD_SIZE)
    query_rotated = lower_precision(apply_rotation(query_projected, cosine_table, sine_values)).reshape(sequence_length, KEY_VALUE_HEADS, QUERY_HEADS // KEY_VALUE_HEADS, HEAD_SIZE)
    key_rot = lower_precision(apply_rotation(key_projected, cosine_table, sine_values))
    attended = lower_precision(lower_backward(attend(query_rotated, key_rot, value_projected)))
    residual = inputs + lower_backward(jnp.dot(attended, output_w, precision=highest_precision))
    mixed_rows = lower_precision(residual * inverse_root(residual) * gain_two)
    logits = jnp.dot(mixed_rows, router_w, precision=highest_precision)
    chosen = jnp.take_along_axis(logits, route_ids, axis=-1)
    gate_weights = jax.nn.softmax(chosen, axis=-1)
    group_rows = SEQ_DEV // N_TP
    group_count = sequence_length // group_rows
    slot_ids = jax.vmap(slots_of)(route_ids.reshape(group_count, group_rows, TOPK)).reshape(sequence_length, TOPK)
    group_of = (jnp.arange(sequence_length, dtype=jnp.int32) // group_rows)[:, None]
    target = (group_of * EXPERTS + route_ids) * CAP + slot_ids
    flat_rows = jnp.zeros((group_count * EXPERTS * CAP, MODEL_DIM), jnp.float32).at[target.reshape(-1)].set(jnp.repeat(mixed_rows, TOPK, axis=0))
    per_expert = flat_rows.reshape(group_count, EXPERTS, CAP, MODEL_DIM).transpose(1, 0, 2, 3).reshape(EXPERTS, group_count * CAP, MODEL_DIM)
    gate_split = gate_w.reshape(MODEL_DIM, EXPERTS, EFF).transpose(1, 0, 2)
    up_split = up_w.reshape(MODEL_DIM, EXPERTS, EFF).transpose(1, 0, 2)
    down_split = down_w.reshape(EXPERTS, EFF, MODEL_DIM)
    expert_out = experts_apply(per_expert, gate_split, up_split, down_split)
    flat_out = expert_out.reshape(EXPERTS, group_count, CAP, MODEL_DIM).transpose(1, 0, 2, 3).reshape(group_count * EXPERTS * CAP, MODEL_DIM)
    picked = flat_out[target]
    return residual + lax.optimization_barrier(jnp.sum(gate_weights[..., None] * picked, axis=1))

def reference(x_in, cotangent, norm1_gain, wq, wk, wv, wo, norm2_gain, router, w_gate, w_up, w_down, routes):
    params = [weight_arr.astype(jnp.float32) for weight_arr in (norm1_gain, wq, wk, wv, wo, norm2_gain, router, w_gate, w_up, w_down)]
    totals = [jnp.zeros_like(weight_arr) for weight_arr in params]
    act_list = []
    grad_list = []
    for micro_index in range(MICRO):
        inputs = x_in[micro_index].astype(jnp.float32)
        pullbacks = []
        outs_micro = []
        for section_index in range(N_SECTION):
            route_ids = routes[section_index, micro_index]

            def section_apply(values, *weights, route_ids=route_ids):
                return layer_forward(values, *weights, route_ids)
            output_val, pullback = jax.vjp(section_apply, inputs, *[weight_arr[section_index] for weight_arr in params])
            pullbacks.append(pullback)
            output_low = output_val.astype(jnp.bfloat16)
            outs_micro.append(output_low)
            inputs = output_low.astype(jnp.float32)
        gradient = cotangent[micro_index].astype(jnp.float32)
        grads_micro = [None] * N_SECTION
        for section_index in range(N_SECTION - 1, -1, -1):
            pieces = pullbacks[section_index](gradient)
            grad_low = pieces[0].astype(jnp.bfloat16)
            grads_micro[section_index] = grad_low
            gradient = grad_low.astype(jnp.float32)
            totals = [total_arr.at[section_index].add(piece_arr) for total_arr, piece_arr in zip(totals, pieces[1:])]
        act_list.append(jnp.stack(outs_micro))
        grad_list.append(jnp.stack(grads_micro))
    activations = jnp.stack(act_list, axis=1)
    input_grads = jnp.stack(grad_list, axis=1)
    return (activations, input_grads, totals[0], totals[1], totals[2], totals[3], totals[4], totals[5], totals[6], totals[7], totals[8], totals[9])
```

```python
import jax
import jax.numpy as jnp
import numpy as np
from jax import lax
from jax.experimental import pallas as pl
from jax.experimental.pallas import tpu as pltpu
from jax.sharding import PartitionSpec as P

HEAD = 64
TOPK = 8
BLOCK = 128
EXPERT_BLOCKS = 4
SIDE = 4
CHIPS = SIDE * SIDE
LANES = 128
SLOTS = 8
GROUP = 32
epsilon = 1e-05
bf16 = jnp.bfloat16
f32 = jnp.float32


def nn(a, b):
    return lax.dot_general(a, b, (((1,), (0,)), ((), ())), preferred_element_type=f32)


def nt(a, b):
    return lax.dot_general(a, b, (((1,), (1,)), ((), ())), preferred_element_type=f32)


def tn(a, b):
    return lax.dot_general(a, b, (((0,), (0,)), ((), ())), preferred_element_type=f32)


def iota(shape, dim):
    return lax.broadcasted_iota(jnp.int32, shape, dim)


def whole_spec(shape, **more):
    return pl.BlockSpec(shape, lambda m: (0,) * len(shape), **more)


def micro_spec(shape):
    return pl.BlockSpec((None, *shape), lambda m: (m, *(0,) * len(shape)))


def local_call(kernel, outs, operands, scratch=(), flops=0, smem=0, vmem=40, each=(), sums=(), micros=1):
    each = list(each)
    moved = sum(int(np.prod(v.shape)) * v.dtype.itemsize for v in [*operands, *each])
    moved += sum(micros * int(np.prod(s)) * jnp.dtype(d).itemsize for s, d in outs)
    params = dict(
        scratch_shapes=[pltpu.VMEM(s, d) for s, d in scratch],
        compiler_params=pltpu.CompilerParams(vmem_limit_bytes=vmem * 1024 * 1024),
        cost_estimate=pl.CostEstimate(flops=flops, bytes_accessed=moved, transcendentals=0),
    )
    scalars = [pl.BlockSpec(memory_space=pltpu.SMEM)] * smem
    if not each:
        return pl.pallas_call(
            kernel,
            out_shape=[jax.ShapeDtypeStruct(s, d) for s, d in outs],
            in_specs=scalars + [pl.BlockSpec(memory_space=pltpu.VMEM)] * (len(operands) - smem),
            out_specs=[pl.BlockSpec(memory_space=pltpu.VMEM)] * len(outs),
            **params,
        )(*operands)
    return pl.pallas_call(
        kernel,
        grid=(micros,),
        out_shape=[jax.ShapeDtypeStruct((micros, *s), d) for s, d in outs]
        + [jax.ShapeDtypeStruct(s, d) for s, d in sums],
        in_specs=scalars
        + [whole_spec(v.shape, pipeline_mode=pl.Buffered(1)) for v in operands[smem:]]
        + [micro_spec(v.shape[1:]) for v in each],
        out_specs=[micro_spec(s) for s, d in outs] + [whole_spec(s) for s, d in sums],
        **params,
    )(*operands, *each)


def turn(values, cosine, sine):
    lane = iota(values.shape, 1) % HEAD
    partner = jnp.where(
        lane < HEAD // 2,
        pltpu.roll(values, LANES - HEAD // 2, 1),
        pltpu.roll(values, HEAD // 2, 1),
    )
    return values * cosine + partner * sine


def project_kernel(x_ref, gain_ref, w_ref, cos_ref, sin_ref, a_ref, q_ref, kv_ref):
    x = x_ref[...].astype(f32)
    root = lax.rsqrt(jnp.mean(x * x, axis=-1, keepdims=True) + epsilon)
    a = (x * root * gain_ref[...]).astype(bf16)
    a_ref[...] = a
    both = nn(a, w_ref[...])
    cosine, sine = cos_ref[...], sin_ref[...]
    for i in range(3):
        at = slice(i * LANES, (i + 1) * LANES)
        q_ref[:, at] = turn(both[:, at], cosine, sine).astype(bf16)
    kv_ref[:, :LANES] = turn(both[:, 3 * LANES : 4 * LANES], cosine, sine).astype(bf16)
    kv_ref[:, LANES:] = both[:, 4 * LANES :].astype(bf16)


def head_rows(values, j):
    pair = values[:, j // 2 * LANES : (j // 2 + 1) * LANES]
    if j % 2 != j // 3:
        pair = pltpu.roll(pair, HEAD, 1)
    low = iota(pair.shape, 1) < HEAD
    return jnp.where(low if j < 3 else jnp.logical_not(low), pair, 0.0)


def spread_heads(source_ref, target_ref, scale):
    rows = source_ref.shape[0]
    values = source_ref[...].astype(f32)
    for j in range(6):
        target_ref[j * rows : (j + 1) * rows, :] = (head_rows(values, j) * scale).astype(bf16)


def join_heads(wide, rows):
    heads = []
    for j in range(6):
        at = HEAD if j >= 3 else 0
        heads.append(wide[at : at + HEAD, j * rows : (j + 1) * rows])
    return [jnp.concatenate(heads[2 * p : 2 * p + 2], axis=0).T for p in range(3)]


def in_reach(row_ref, kb, rows, shape):
    ahead = iota((rows, shape[1]), 1) % rows - iota((rows, shape[1]), 0)
    count = shape[0] // rows
    parts = [ahead + (row_ref[0] - row_ref[1 + kb * count + i]) >= 0 for i in range(count)]
    return jnp.concatenate(parts, axis=0)


def attend_kernel(
    row_ref, wo_ref, q_ref, kv0, kv1, kv2, kv3, o_ref, l_ref, y_ref, qp, st
):
    rows = q_ref.shape[0]
    step = kv0.shape[0]
    spread_heads(q_ref, qp, 0.125)
    peak = None
    for kb, kv_ref in enumerate((kv0, kv1, kv2, kv3)):
        s = nt(kv_ref[:, :LANES], qp[...])
        s = jnp.where(in_reach(row_ref, kb, rows, s.shape), s, -1e30)
        st[kb * step : (kb + 1) * step, :] = s
        top = jnp.max(s, axis=0, keepdims=True)
        peak = top if peak is None else jnp.maximum(peak, top)
    total, wide = 0.0, 0.0
    for kb, kv_ref in enumerate((kv0, kv1, kv2, kv3)):
        p = jnp.exp(st[kb * step : (kb + 1) * step, :] - peak)
        total = total + jnp.sum(p, axis=0, keepdims=True)
        wide = wide + tn(kv_ref[:, LANES:], p.astype(bf16))
    wide = wide / total
    l_ref[...] = jnp.broadcast_to(peak + jnp.log(total), l_ref.shape)
    for p, part in enumerate(join_heads(wide, rows)):
        o_ref[:, p * LANES : (p + 1) * LANES] = part.astype(bf16)
    y_ref[...] = nn(o_ref[...], wo_ref[...]).astype(bf16)


def attend_back_kernel(
    row_ref, wo_ref, cos_ref, sin_ref, q_ref, kv0, kv1, kv2, kv3, da_ref, l_ref, o_ref,
    dq_ref, dkv0, dkv1, dkv2, dkv3, qp, dp, dob, prod,
):
    rows = q_ref.shape[0]
    spread_heads(q_ref, qp, 0.125)
    dob[...] = nt(da_ref[...], wo_ref[...]).astype(bf16)
    spread_heads(dob, dp, 1.0)
    both = dob[...].astype(f32) * o_ref[...].astype(f32)
    for j in range(6):
        prod[j * rows : (j + 1) * rows, :] = head_rows(both, j)
    inner = lax.dot_general(
        jnp.ones((8, LANES), f32),
        prod[...],
        (((1,), (1,)), ((), ())),
        precision=lax.Precision.HIGHEST,
        preferred_element_type=f32,
    )[0:1, :]
    log_total = l_ref[0:1, :]
    wide = 0.0
    for kb, (kv_ref, dkv_ref) in enumerate(((kv0, dkv0), (kv1, dkv1), (kv2, dkv2), (kv3, dkv3))):
        keys_here, values_here = kv_ref[:, :LANES], kv_ref[:, LANES:]
        s = nt(keys_here, qp[...])
        p = jnp.where(in_reach(row_ref, kb, rows, s.shape), jnp.exp(s - log_total), 0.0)
        ds = (p * (nt(values_here, dp[...]) - inner)).astype(bf16)
        dkv_ref[:, :LANES] = nn(ds, qp[...]).astype(bf16)
        dkv_ref[:, LANES:] = nn(p.astype(bf16), dp[...]).astype(bf16)
        wide = wide + tn(keys_here, ds)
    for p, part in enumerate(join_heads(wide * 0.125, rows)):
        dq_ref[:, p * LANES : (p + 1) * LANES] = turn(part, cos_ref[...], -sin_ref[...]).astype(bf16)


def after_keys_kernel(
    dkv0, dkv1, dkv2, dkv3, dq_ref, x_ref, w_ref, cos_ref, sin_ref, g_ref, y_ref, gain_ref
):
    whole = dkv0[...].astype(f32) + dkv1[...].astype(f32)
    whole = whole + (dkv2[...].astype(f32) + dkv3[...].astype(f32))
    g_ref[:, : 3 * LANES] = dq_ref[...]
    g_ref[:, 3 * LANES : 4 * LANES] = turn(whole[:, :LANES], cos_ref[...], -sin_ref[...]).astype(bf16)
    g_ref[:, 4 * LANES :] = whole[:, LANES:].astype(bf16)
    y = nt(g_ref[...], w_ref[...])
    y_ref[...] = y.astype(bf16)
    x = x_ref[...].astype(f32)
    root = lax.rsqrt(jnp.mean(x * x, axis=-1, keepdims=True) + epsilon)
    gain_ref[...] = jnp.broadcast_to(jnp.sum(y * (x * root), axis=0, keepdims=True), gain_ref.shape)


CHUNK = 256
HALF = CHUNK // GROUP * SLOTS


def picks(tgt_ref, ch):
    at = slice(ch * CHUNK, (ch + 1) * CHUNK)
    rows = iota((HALF, CHUNK), 0)
    return rows == tgt_ref[0:1, at], rows == tgt_ref[1:2, at]


def one_hot(pick_a, pick_b):
    return jnp.concatenate([pick_a.astype(f32), pick_b.astype(f32)], axis=0).astype(bf16)


def row_of(table, expert):
    return jnp.sum(jnp.where(iota(table.shape, 0) == expert, table, 0.0), axis=0, keepdims=True)


def two_of(refs, ch):
    return jnp.concatenate([refs[2 * ch][...], refs[2 * ch + 1][...]], axis=0)


def put_two(refs, ch, value):
    rows = value.shape[0] // 2
    refs[2 * ch][...] = value[:rows]
    refs[2 * ch + 1][...] = value[rows:]


def experts_kernel(s_ref, router, wg, wu, wd, *refs):
    tokens_in, refs = refs[: 2 * SIDE], refs[2 * SIDE :]
    tgt, mask, *refs = refs
    tokens_out, refs = refs[: 2 * SIDE], refs[2 * SIDE :]
    gates, slots_in, g_ref, u_ref, hidden, weights, scaled = refs
    chunks = SIDE
    for ch in range(chunks):
        at = slice(ch * CHUNK, (ch + 1) * CHUNK)
        z = nt(router[...], two_of(tokens_in, ch))
        chosen = mask[:, at]
        z = jnp.where(chosen > 0.0, z, -1e30)
        e = jnp.exp(z - jnp.max(z, axis=0, keepdims=True)) * chosen
        gates[:, at] = e / jnp.sum(e, axis=0, keepdims=True)
    rows = slots_in.shape[0] // 2
    for ch in range(chunks):
        pick_a, pick_b = picks(tgt, ch)
        got = nn(one_hot(pick_a, pick_b), two_of(tokens_in, ch)).astype(bf16)
        here = gates[:, ch * CHUNK : (ch + 1) * CHUNK]
        for which, pick in enumerate((pick_a, pick_b)):
            at = which * rows + ch * HALF
            slots_in[at : at + HALF, :] = got[which * HALF : (which + 1) * HALF]
            weight = jnp.sum(jnp.where(pick, row_of(here, s_ref[which]), 0.0), axis=1, keepdims=True)
            weights[at : at + HALF, :] = jnp.broadcast_to(weight, (HALF, LANES))
    hidden[...] = jnp.zeros_like(hidden)
    for k in range(wg.shape[1] // BLOCK):
        at = slice(k * BLOCK, (k + 1) * BLOCK)
        here = pl.ds(pl.multiple_of(s_ref[2 + k] * rows, rows), rows)
        both = nn(slots_in[here, :], jnp.concatenate([wg[:, at], wu[:, at]], axis=1))
        g, u = both[:, :BLOCK], both[:, BLOCK:]
        g_ref[:, at] = g
        u_ref[:, at] = u
        hidden[here, at] = (g * jax.nn.sigmoid(g) * u).astype(bf16)
    for at in range(0, wd.shape[1], CHUNK):
        part = nn(hidden[...], wd[:, at : at + CHUNK])
        scaled[:, at : at + CHUNK] = (part * weights[:, 0:1]).astype(bf16)
    for ch in range(chunks):
        at = ch * HALF
        both = jnp.concatenate([scaled[at : at + HALF], scaled[rows + at : rows + at + HALF]], axis=0)
        put_two(tokens_out, ch, tn(one_hot(*picks(tgt, ch)), both).astype(bf16))


def experts_back_kernel(s_ref, router, wg, wu, wd, *refs):
    grads_in, refs = refs[: 2 * SIDE], refs[2 * SIDE :]
    tokens_in, refs = refs[: 2 * SIDE], refs[2 * SIDE :]
    tgt, gates, g_ref, u_ref, *refs = refs
    grads_out, refs = refs[: 2 * SIDE], refs[2 * SIDE :]
    dgu_ref, h_ref, dy, router_grad, inner, back = refs
    chunks = SIDE
    rows = dy.shape[0] // 2
    for ch in range(chunks):
        pick_a, pick_b = picks(tgt, ch)
        here = gates[:, ch * CHUNK : (ch + 1) * CHUNK]
        got = nn(one_hot(pick_a, pick_b), two_of(grads_in, ch))
        for which, pick in enumerate((pick_a, pick_b)):
            weight = jnp.sum(jnp.where(pick, row_of(here, s_ref[which]), 0.0), axis=1, keepdims=True)
            at = which * rows + ch * HALF
            dy[at : at + HALF, :] = (got[which * HALF : (which + 1) * HALF] * weight).astype(bf16)
    inner[...] = jnp.zeros_like(inner)
    back[...] = jnp.zeros_like(back)
    for k in range(wg.shape[1] // BLOCK):
        at = slice(k * BLOCK, (k + 1) * BLOCK)
        here = pl.ds(pl.multiple_of(s_ref[2 + k] * rows, rows), rows)
        dh = nt(dy[here, :], wd[at, :])
        g, u = g_ref[:, at], u_ref[:, at]
        sig = jax.nn.sigmoid(g)
        swish = g * sig
        h = (swish * u).astype(bf16)
        h_ref[:, at] = h
        inner[here, :] += jnp.broadcast_to(
            jnp.sum(h.astype(f32) * dh, axis=1, keepdims=True), (rows, LANES)
        )
        dg = (dh * u * sig * (1.0 + g * (1.0 - sig))).astype(bf16)
        du = (dh * swish).astype(bf16)
        both = jnp.concatenate([dg, du], axis=1)
        dgu_ref[:, 2 * k * BLOCK : 2 * (k + 1) * BLOCK] = both
        back[here, :] += nt(both, jnp.concatenate([wg[:, at], wu[:, at]], axis=1))
    for ch in range(chunks):
        pick_a, pick_b = picks(tgt, ch)
        span = slice(ch * CHUNK, (ch + 1) * CHUNK)
        sums = []
        for which, pick in enumerate((pick_a, pick_b)):
            at = which * rows + ch * HALF
            column = inner[at : at + HALF, 0:1]
            sums.append(jnp.sum(jnp.where(pick, column, 0.0), axis=0, keepdims=True))
        table = gates[:, span]
        expert = iota(table.shape, 0)
        dz = jnp.where(expert == s_ref[0], sums[0], 0.0) + jnp.where(expert == s_ref[1], sums[1], 0.0)
        dz = dz - table * (sums[0] + sums[1])
        high = dz.astype(bf16)
        lower = (dz - high.astype(f32)).astype(bf16)
        both = jnp.concatenate([high, lower], axis=0)
        at = ch * HALF
        moved = jnp.concatenate([back[at : at + HALF, :], back[rows + at : rows + at + HALF, :]], axis=0)
        value = tn(
            jnp.concatenate([one_hot(pick_a, pick_b), high], axis=0),
            jnp.concatenate([moved.astype(bf16), router[...]], axis=0),
        )
        put_two(grads_out, ch, value.astype(bf16))
        part = nn(both, two_of(tokens_in, ch))
        part = part[: table.shape[0]] + part[table.shape[0] :]
        if ch == 0:
            begin = pl.program_id(0) == 0
            router_grad[...] = part + jnp.where(begin, 0.0, router_grad[...])
        else:
            router_grad[...] += part


def expert_weights_kernel(s_ref, b_own, o0, o1, o2, o3, g_own, g_other, h, dy, gate, up, down):
    rows, size = h.shape[0], o0.shape[0]
    begin = pl.program_id(0) == 0
    for k in range(h.shape[1] // BLOCK):
        at = slice(k * BLOCK, (k + 1) * BLOCK)
        wide = slice(2 * k * BLOCK, 2 * (k + 1) * BLOCK)
        here = pl.ds(pl.multiple_of(s_ref[2 + k] * rows, rows), rows)
        first = s_ref[2 + k] == 0
        theirs = [jnp.where(first, o0[...], o2[...]), jnp.where(first, o1[...], o3[...])]
        both = tn(
            jnp.concatenate([b_own[here, :], *theirs], axis=0),
            jnp.concatenate([g_own[:, wide], g_other[:, wide]], axis=0),
        )
        low = tn(h[:, at], dy[here, :])
        gate[:, at] = both[:, :BLOCK] + jnp.where(begin, 0.0, gate[:, at])
        up[:, at] = both[:, BLOCK:] + jnp.where(begin, 0.0, up[:, at])
        down[at, :] = low + jnp.where(begin, 0.0, down[at, :])


def ring(stage, steps):
    pairs = []
    for x in range(SIDE):
        for z in range(SIDE):
            for core in range(2):
                along_x = (core == 0) == (stage == 0)
                to = ((x + steps) % SIDE, z) if along_x else (x, (z + steps) % SIDE)
                pairs.append(((x * SIDE + z) * 2 + core, (to[0] * SIDE + to[1]) * 2 + core))
    return pairs


def other_core(value):
    return lax.ppermute(value, "ep", [(i, i ^ 1) for i in range(2 * CHIPS)])


def other_half(value):
    return lax.ppermute(value, "tp", [(0, 1), (1, 0)])


def other_both(value):
    pairs = [(2 * i + t, 2 * (i ^ 1) + 1 - t) for i in range(2 * CHIPS) for t in range(2)]
    return lax.ppermute(value, ("ep", "tp"), pairs)


def in_order(own, other, place, dim):
    return jnp.concatenate(
        [jnp.where(place == 0, own, other), jnp.where(place == 0, other, own)], axis=dim
    )


def from_ring(value, stage):
    return [value] + [lax.ppermute(value, "ep", ring(stage, -d)) for d in range(1, SIDE)]


def to_ring(pieces, stage):
    return [pieces[0]] + [
        lax.ppermute(pieces[d], "ep", ring(stage, d)) for d in range(1, SIDE)
    ]


def everyone(value):
    return from_ring(jnp.concatenate(from_ring(value, 0), axis=1), 1)


def added(pieces):
    pieces = [p.astype(f32) for p in pieces]
    return (pieces[0] + pieces[1]) + (pieces[2] + pieces[3])


def pieces_of(value):
    size = value.shape[1] // SIDE
    return [value[:, d * size : (d + 1) * size] for d in range(SIDE)]


def to_owners(pieces, beside=()):
    joined, *beside = pin(added(to_ring(pieces, 1)).astype(bf16), *beside)
    return to_ring(pieces_of(joined), 0), beside


def pin(*values):
    return lax.optimization_barrier(values)


SAME_CORE = [[2 * chip + core for chip in range(CHIPS)] for core in range(2)]


def exchange(pieces, groups=SAME_CORE):
    return lax.all_to_all(pieces, "ep", 0, 0, tiled=True, axis_index_groups=groups)


def broadcast(value, count=CHIPS, groups=SAME_CORE):
    return exchange(jnp.broadcast_to(value[None], (count, *value.shape)), groups)


def half_of(value, place, dim=0):
    size = value.shape[dim] // 2
    mine = lax.dynamic_slice_in_dim(value, place * size, size, dim)
    rest = lax.dynamic_slice_in_dim(value, (1 - place) * size, size, dim)
    return mine, rest


def body(
    x_in, cotangent, norm1_gain, wq, wk, wv, wo, norm2_gain, router, w_gate, w_up, w_down, routes
):
    section = lax.axis_index("section")
    rank = lax.axis_index("ep")
    half = lax.axis_index("tp")
    chip, core = rank // 2, rank % 2
    x, z = chip // SIDE, chip % SIDE
    micros, core_rows, width = x_in.shape
    own_rows = core_rows // 2
    chip_rows = core_rows * 2
    length = chip_rows * CHIPS
    experts = router.shape[2]
    blocks = w_gate.shape[2] // BLOCK
    gain_one = norm1_gain.reshape(1, width)
    gain_two = norm2_gain.reshape(1, width)
    gate_w, up_w, down_w = w_gate[0], w_up[0], w_down[0]
    expert_rows = -(-experts // 16) * 16
    router_t = jnp.pad(router[0].T, ((0, expert_rows - experts), (0, 0)))

    qkv_w = jnp.concatenate([half_of(w[0], core, 1)[0] for w in (wq, wk, wv)], axis=1)
    out_w = half_of(wo[0], core)[0]

    first_row = (chip * chip_rows).astype(jnp.int32)
    positions = (first_row + jnp.arange(chip_rows, dtype=jnp.int32)).astype(f32)
    quarter = HEAD // 2
    frequency = 10000.0 ** (-jnp.arange(quarter, dtype=f32) * 2.0 / HEAD)
    phase = positions[:, None] * frequency[None, :]
    cosine = jnp.tile(jnp.cos(phase), (1, 4))
    sine = jnp.concatenate([-jnp.sin(phase), jnp.sin(phase)] * 2, axis=1)

    def chips_met(which_core):
        inner, outer = jnp.arange(CHIPS) % SIDE, jnp.arange(CHIPS) // SIDE
        by_x = jnp.where(which_core == 0, inner, outer)
        by_z = jnp.where(which_core == 0, outer, inner)
        return ((x + by_x) % SIDE) * SIDE + (z + by_z) % SIDE

    row_scalars = jnp.concatenate(
        [first_row.reshape(1), chips_met(core) * chip_rows]
    ).astype(jnp.int32)

    first_expert = rank * blocks // EXPERT_BLOCKS
    which = (rank * blocks + jnp.arange(blocks)) // EXPERT_BLOCKS - first_expert
    scalars = jnp.concatenate(
        [jnp.stack([first_expert, first_expert + 1]), which]
    ).astype(jnp.int32)

    tokens = CHIPS * own_rows
    slot_rows = 2 * 2 * CHIPS * SLOTS
    hidden_width = blocks * BLOCK
    both_rows = micros * chip_rows
    cosines, sines = jnp.tile(cosine, (micros, 1)), jnp.tile(sine, (micros, 1))

    def prepare(own_routes):
        all_routes = broadcast(own_routes.reshape(-1, LANES), 2 * CHIPS, None)
        met = jnp.concatenate([chips_met(core) * 2 + core, chips_met(1 - core) * 2 + 1 - core])
        all_routes = jnp.take(all_routes, met, axis=0)
        both_routes = all_routes.reshape(2 * CHIPS, micros, own_rows, TOPK).transpose(1, 0, 2, 3)
        both_routes = both_routes.reshape(micros, 2 * CHIPS * own_rows, TOPK)
        named = (
            both_routes[:, None, :, :] == jnp.arange(expert_rows, dtype=jnp.int32)[None, :, None, None]
        )
        masks = jnp.any(named, axis=-1).astype(f32)
        wanted = jnp.stack([first_expert, first_expert + 1]).astype(jnp.int32)
        hits = jnp.any(both_routes[:, None, :, :] == wanted[None, :, None, None], axis=-1)
        hits = hits.reshape(micros, 2, 2 * CHIPS, own_rows).astype(jnp.int32)
        before = jnp.cumsum(hits, axis=-1) - hits
        base = (jnp.arange(2 * CHIPS, dtype=jnp.int32) % (CHUNK // GROUP)) * SLOTS
        targets = jnp.where(hits > 0, base[None, None, :, None] + before, -1)
        targets = targets.reshape(micros, 2, 2 * CHIPS * own_rows)
        return targets, masks

    def project(x128):
        a, q, kv = local_call(
            project_kernel,
            [((both_rows, width), bf16), ((both_rows, 3 * LANES), bf16), ((both_rows, 2 * LANES), bf16)],
            [x128.reshape(both_rows, width), gain_one, qkv_w, cosines, sines],
            flops=2 * both_rows * width * 5 * LANES,
            vmem=16,
        )
        return a, q.reshape(micros, chip_rows, -1), kv.reshape(micros, chip_rows, -1)

    def attend(q, kv):
        return local_call(
            attend_kernel,
            [((chip_rows, 3 * LANES), bf16), ((8, 6 * chip_rows), f32), ((chip_rows, width), bf16)],
            [row_scalars, out_w],
            each=[q, *kv],
            scratch=[((6 * chip_rows, LANES), bf16), ((length, 6 * chip_rows), f32)],
            flops=8 * micros * length * 6 * chip_rows * LANES,
            smem=1,
            vmem=32,
            micros=micros,
        )

    def attend_back(q, kv, grad, log_total, o):
        return local_call(
            attend_back_kernel,
            [((chip_rows, 3 * LANES), bf16)] + [((length // SIDE, 2 * LANES), bf16)] * SIDE,
            [row_scalars, out_w, cosine, sine],
            each=[q, *kv, grad, log_total, o],
            scratch=[
                ((6 * chip_rows, LANES), bf16),
                ((6 * chip_rows, LANES), bf16),
                ((chip_rows, 3 * LANES), bf16),
                ((6 * chip_rows, LANES), f32),
            ],
            flops=20 * micros * length * 6 * chip_rows * LANES,
            smem=1,
            vmem=32,
            micros=micros,
        )

    def after_keys(arrived, dq, x128):
        dqkv, y, gain = local_call(
            after_keys_kernel,
            [((both_rows, 5 * LANES), bf16), ((both_rows, width), bf16), ((8, width), f32)],
            [v.reshape(both_rows, -1) for v in (*arrived, dq, x128)] + [qkv_w, cosines, sines],
            flops=2 * both_rows * width * 5 * LANES,
            vmem=16,
        )
        return dqkv, y.reshape(micros, chip_rows, width), gain[:1]

    piece = ((tokens // SIDE, width), bf16)

    def run_experts(arrived):
        result = local_call(
            experts_kernel,
            [piece] * (2 * SIDE)
            + [
                ((expert_rows, 2 * tokens), f32),
                ((slot_rows, width), bf16),
                ((slot_rows // 2, hidden_width), f32),
                ((slot_rows // 2, hidden_width), f32),
            ],
            [scalars, router_t, gate_w, up_w, down_w],
            each=[*arrived, targets, masks],
            scratch=[
                ((slot_rows, hidden_width), bf16),
                ((slot_rows, LANES), f32),
                ((slot_rows, width), bf16),
            ],
            flops=10 * micros * slot_rows * hidden_width * width,
            smem=1,
            vmem=48,
            micros=micros,
        )
        return result[: 2 * SIDE], result[2 * SIDE :]

    def run_experts_back(grads, arrived, gates, g, u):
        result = local_call(
            experts_back_kernel,
            [piece] * (2 * SIDE)
            + [
                ((slot_rows // 2, 2 * hidden_width), bf16),
                ((slot_rows // 2, hidden_width), bf16),
                ((slot_rows, width), bf16),
            ],
            [scalars, router_t, gate_w, up_w, down_w],
            each=[*grads, *arrived, targets, gates, g, u],
            sums=[((expert_rows, width), f32)],
            scratch=[((slot_rows, LANES), f32), ((slot_rows, width), f32)],
            flops=10 * micros * slot_rows * hidden_width * width,
            smem=1,
            vmem=52,
            micros=micros,
        )
        return result[: 2 * SIDE], result[2 * SIDE :]

    def sum_four(part):
        mine, rest = half_of(part, core, 1)
        mine, rest = half_of(mine.astype(f32) + other_core(rest).astype(f32), half, 1)
        return mine + other_half(rest.astype(bf16)).astype(f32)

    def to_four(rows32):
        rows64 = in_order(rows32, other_half(rows32), half, 1)
        return in_order(rows64, other_core(rows64), core, 1)

    def tokens_out(rows32):
        arrived = everyone(rows32)
        return arrived + [other_core(p) for p in arrived]

    def over_cores(parts):
        return [
            (own.astype(f32) + other_core(other).astype(f32)).astype(bf16)
            for own, other in zip(parts[:SIDE], parts[SIDE:])
        ]

    def tokens_back(parts, beside=()):
        pieces, beside = to_owners(over_cores(parts), beside)
        return added(pieces), beside

    def inverse_root(values):
        return lax.rsqrt(jnp.mean(values * values, axis=-1, keepdims=True) + epsilon)

    def norm_back(values, root, gradient, gain):
        weighted = gradient * gain
        return root * weighted - values * root**3 * jnp.mean(weighted * values, axis=-1, keepdims=True)

    def forward(own, x128, sent=None):
        nonlocal targets, masks
        a, q, kv = project(x128)
        if sent is not None:
            kv, own_routes = pin(
                kv, lax.dynamic_slice_in_dim(routes[0], half * own_rows, own_rows, 1)
            )
            targets, masks = prepare(own_routes)
        kv_all = everyone(kv)
        if sent is not None:
            *kv_all, targets, masks = pin(*kv_all, targets, masks)
        o, log_total, y = attend(q, kv_all)
        residual = own.astype(f32) + sum_four(y)
        mixed = (residual * inverse_root(residual) * gain_two).astype(bf16)
        arrived = tokens_out(mixed if sent is None else jnp.where(section == 0, mixed, sent))
        parts, rest = run_experts(arrived)
        return parts, (own, x128, a, q, kv_all, o, log_total, residual, arrived, *rest)

    def backward(grad_rows, grads, kept, first=(), second=()):
        residual, arrived, gates, _, g, u = kept[7:]
        parts, (dgu, h, dy, router_grad) = run_experts_back(grads, arrived, gates, g, u)
        *parts, first = pin(*parts, first)
        if second:
            *parts, rows = pin(*parts, second[0])
            second = [other_half(rows)]
        mixed_grad, second = tokens_back(parts, second)
        root = inverse_root(residual)
        gain_two_grad = jnp.sum(mixed_grad * residual * root, axis=(0, 1))
        resid_grad = grad_rows.astype(f32) + norm_back(residual, root, mixed_grad, gain_two)
        return resid_grad, (dgu, h, dy), router_grad, gain_two_grad, [first, *second]

    targets = masks = None
    own_x = lax.dynamic_slice_in_dim(x_in, half * own_rows, own_rows, 1)
    x128 = in_order(x_in, other_core(x_in), core, 1)
    parts, kept = forward(own_x, x128, cotangent)
    upper_grads = kept[8]
    out = (kept[7] + tokens_back(parts)[0]).astype(bf16)
    same = lax.ppermute(out, "section", [(0, 1)])
    rows64 = in_order(same, lax.ppermute(out, ("section", "tp"), [(0, 3), (1, 2)]), half, 1)
    whole = in_order(rows64, other_core(rows64), core, 1)
    last_parts, kept = forward(
        jnp.where(section == 0, own_x, same), jnp.where(section == 0, x128, whole)
    )
    own, x128, a, q, kv_all, o, log_total, residual = kept[:8]
    own, slots_in = own.astype(f32), kept[10]

    resid_grad, *_ = backward(cotangent, upper_grads, kept)
    low, *joined = pin(resid_grad.astype(bf16), *over_cores(last_parts))
    pieces = to_ring(joined, 1)
    dq, *dkv = attend_back(q, kv_all, to_four(low), log_total, o)
    *dkv, joined = pin(*dkv, added(pieces).astype(bf16))
    dkv, _ = to_owners(dkv)
    *dkv, joined = pin(*dkv, joined)
    pieces = to_ring(pieces_of(joined), 0)
    _, y, _ = after_keys(dkv, dq, x128)
    normed_grad, out = pin(sum_four(y), (residual + added(pieces)).astype(bf16))
    root = inverse_root(own)
    upper = (resid_grad + norm_back(own, root, normed_grad, gain_one)).astype(bf16)
    coming = lax.ppermute(upper, "section", [(1, 0)])
    coming, other_out = pin(jnp.where(section == 0, coming, cotangent), other_half(out))
    activations = in_order(out, other_out, half, 1)

    size = slot_rows // SIDE
    other_slots = []

    def next_slots(*values):
        at = len(other_slots) * size
        *values, rows = pin(*values, slots_in[:, at : at + size])
        other_slots.append(other_half(rows))
        return values

    def slots_done(*values):
        *values, other_slots[-1] = pin(*values, other_slots[-1])
        return values

    (coming,) = next_slots(coming)
    arrived = from_ring(coming, 0)
    (arrived,) = next_slots(*slots_done(jnp.concatenate(arrived, axis=1)))
    arrived = next_slots(*slots_done(*from_ring(arrived, 1)))
    grads = arrived + [other_core(p) for p in arrived]
    resid_grad, (dgu, h, dy), router_grad, gain_two_grad, last_slots = backward(
        coming, grads, kept, other_slots[2], [slots_in[:, 3 * size :]]
    )
    other_slots[2:] = last_slots
    out_grad, dgu_sent = pin(to_four(resid_grad.astype(bf16)), dgu)
    other_dgu = other_half(dgu_sent)
    out_w_grad = tn(o.reshape(both_rows, -1), out_grad.reshape(both_rows, width)).astype(bf16)
    out_w_grad = jnp.sum(
        exchange(out_w_grad.reshape(CHIPS, -1, width)).astype(f32), axis=0
    ).astype(bf16)
    dq, *dkv = attend_back(q, kv_all, out_grad, log_total, o)
    *dkv, out_w_grad, other_dgu = pin(*dkv, out_w_grad, other_dgu)
    all_out = lax.all_gather(out_w_grad, "ep")
    q_grad = tn(a, dq.reshape(both_rows, -1)).astype(bf16).reshape(CHIPS, -1, 3 * LANES)
    q_grad = exchange(q_grad)
    gate_grad, up_grad, down_part = local_call(
        expert_weights_kernel,
        [],
        [scalars],
        each=[slots_in, *other_slots, dgu, other_dgu, h, dy],
        sums=[((width, hidden_width), f32), ((width, hidden_width), f32), ((hidden_width, width), f32)],
        flops=10 * slot_rows * hidden_width * width,
        smem=1,
        vmem=56,
        micros=micros,
    )
    down_part = down_part.astype(bf16)
    arrived, (gate_grad, up_grad, down_part, q_grad) = to_owners(
        dkv, (gate_grad, up_grad, down_part, q_grad)
    )
    other_down = other_half(down_part)
    q_grad = jnp.sum(q_grad.astype(f32), axis=0).astype(bf16)
    dqkv, y, gain_one_grad = after_keys(arrived, dq, x128)
    small = jnp.concatenate([router_grad[:experts], gain_one_grad, gain_two_grad[None]], axis=0)
    kv_width, all_width = 2 * LANES, 5 * LANES
    small_count = small.size
    per_chip = -(-small_count // (CHIPS * 8 * LANES)) * 8 * LANES
    small = jnp.pad(small.reshape(-1), (0, CHIPS * per_chip - small_count)).astype(bf16)
    kv_grad = tn(a, dqkv[:, 3 * LANES :]).astype(bf16).reshape(CHIPS, -1, kv_width)
    lines = kv_grad.shape[1]
    summed = exchange(
        jnp.concatenate([kv_grad, small.reshape(CHIPS, -1, kv_width)], axis=1)
    )
    summed, all_out, q_grad, y = pin(summed, all_out, q_grad, y)
    summed = jnp.sum(summed.astype(f32), axis=0).astype(bf16)
    small = jnp.pad(
        summed[lines:].reshape(-1, LANES), ((0, -per_chip // LANES % 5), (0, 0))
    ).reshape(-1, all_width)
    wide = jnp.concatenate(
        [jnp.concatenate([q_grad, summed[:lines]], axis=1), small], axis=0
    )
    normed_grad = sum_four(y)
    wide, normed_grad, other_down = pin(broadcast(wide), normed_grad, other_down)
    input_grads = (resid_grad + norm_back(own, root, normed_grad, gain_one)).astype(bf16)
    down_grad = down_part.astype(f32) + other_down.astype(f32)
    small = wide[:, lines:].reshape(CHIPS, -1)[:, :per_chip].reshape(-1)[:small_count]
    small = small.reshape(experts + 2, width)
    small = small.astype(f32) + other_core(small).astype(f32)
    small = small + other_half(small.astype(bf16)).astype(f32)
    wide = wide[:, :lines].reshape(width, all_width)
    other_wide = other_core(wide)

    def both_cores(start, end):
        return in_order(wide[:, start:end], other_wide[:, start:end], core, 1).astype(f32)

    grad_q = both_cores(0, 3 * LANES)
    grad_k = both_cores(3 * LANES, 4 * LANES)
    grad_v = both_cores(4 * LANES, 5 * LANES)
    all_out = all_out.reshape(CHIPS, 2, -1, width)
    grad_out = jnp.concatenate(
        [all_out[:, c].reshape(-1, width) for c in range(2)], axis=0
    ).astype(f32)
    return (
        activations[None],
        input_grads[None],
        small[experts][None],
        grad_q[None],
        grad_k[None],
        grad_v[None],
        grad_out[None],
        small[experts + 1][None],
        small[:experts].T[None],
        gate_grad[None],
        up_grad[None],
        down_grad[None],
    )


def solution(mesh):
    ep = "ep"
    ep_tp = ("ep", "tp")
    placed = (
        P(None, ep, None),
        P(None, ep_tp, None),
        P("section", None),
        P("section", None, "tp"),
        P("section", None, "tp"),
        P("section", None, "tp"),
        P("section", "tp", None),
        P("section", None),
        P("section", None, None),
        P("section", None, ep),
        P("section", None, ep),
        P("section", ep, None),
        P("section", None, ep, None),
    )
    return jax.shard_map(
        body,
        mesh=mesh,
        in_specs=placed,
        out_specs=(
            P("section", None, ep, None),
            P("section", None, ep_tp, None),
            P("section", None),
            P("section", None, "tp"),
            P("section", None, "tp"),
            P("section", None, "tp"),
            P("section", "tp", None),
            P("section", None),
            P("section", None, None),
            P("section", None, ep),
            P("section", None, ep),
            P("section", ep, None),
        ),
        check_vma=False,
    )
```

```python
import jax
import jax.numpy as jnp
import numpy as np
from jax import lax
from jax.experimental import pallas as pl
from jax.experimental.pallas import tpu as pltpu
from jax.sharding import PartitionSpec as P

HEAD = 64
TOPK = 8
BLOCK = 128
EXPERT_BLOCKS = 4
SIDE = 4
CHIPS = SIDE * SIDE
LANES = 128
SLOTS = 8
GROUP = 32
epsilon = 1e-05
bf16 = jnp.bfloat16
f32 = jnp.float32


def nn(a, b):
    return lax.dot_general(a, b, (((1,), (0,)), ((), ())), preferred_element_type=f32)


def nt(a, b):
    return lax.dot_general(a, b, (((1,), (1,)), ((), ())), preferred_element_type=f32)


def tn(a, b):
    return lax.dot_general(a, b, (((0,), (0,)), ((), ())), preferred_element_type=f32)


def iota(shape, dim):
    return lax.broadcasted_iota(jnp.int32, shape, dim)


def whole_spec(shape, **more):
    return pl.BlockSpec(shape, lambda m: (0,) * len(shape), **more)


def micro_spec(shape):
    return pl.BlockSpec((None, *shape), lambda m: (m, *(0,) * len(shape)))


def pair_spec(shape):
    return pl.BlockSpec((shape[0], None, *shape[2:]), lambda m: (0, m, *(0,) * len(shape[2:])))


def local_call(
    kernel, outs, operands, scratch=(), flops=0, smem=0, vmem=40, each=(), pairs=(), sums=(), micros=1
):
    each, pairs = list(each), list(pairs)
    moved = sum(int(np.prod(v.shape)) * v.dtype.itemsize for v in [*operands, *each, *pairs])
    moved += sum(micros * int(np.prod(s)) * jnp.dtype(d).itemsize for s, d in outs)
    params = dict(
        scratch_shapes=[pltpu.VMEM(s, d) for s, d in scratch],
        compiler_params=pltpu.CompilerParams(vmem_limit_bytes=vmem * 1024 * 1024),
        cost_estimate=pl.CostEstimate(flops=flops, bytes_accessed=moved, transcendentals=0),
    )
    scalars = [pl.BlockSpec(memory_space=pltpu.SMEM)] * smem
    if not each:
        return pl.pallas_call(
            kernel,
            out_shape=[jax.ShapeDtypeStruct(s, d) for s, d in outs],
            in_specs=scalars + [pl.BlockSpec(memory_space=pltpu.VMEM)] * (len(operands) - smem),
            out_specs=[pl.BlockSpec(memory_space=pltpu.VMEM)] * len(outs),
            **params,
        )(*operands)
    return pl.pallas_call(
        kernel,
        grid=(micros,),
        out_shape=[jax.ShapeDtypeStruct((micros, *s), d) for s, d in outs]
        + [jax.ShapeDtypeStruct(s, d) for s, d in sums],
        in_specs=scalars
        + [whole_spec(v.shape, pipeline_mode=pl.Buffered(1)) for v in operands[smem:]]
        + [micro_spec(v.shape[1:]) for v in each]
        + [pair_spec(v.shape) for v in pairs],
        out_specs=[micro_spec(s) for s, d in outs] + [whole_spec(s) for s, d in sums],
        **params,
    )(*operands, *each, *pairs)


def turn(values, cosine, sine):
    lane = iota(values.shape, 1) % HEAD
    partner = jnp.where(
        lane < HEAD // 2,
        pltpu.roll(values, LANES - HEAD // 2, 1),
        pltpu.roll(values, HEAD // 2, 1),
    )
    return values * cosine + partner * sine


def project_kernel(x_ref, gain_ref, w_ref, cos_ref, sin_ref, a_ref, q_ref, kv_ref):
    x = x_ref[...].astype(f32)
    root = lax.rsqrt(jnp.mean(x * x, axis=-1, keepdims=True) + epsilon)
    a = (x * root * gain_ref[...]).astype(bf16)
    a_ref[...] = a
    both = nn(a, w_ref[...])
    cosine, sine = cos_ref[...], sin_ref[...]
    for i in range(3):
        at = slice(i * LANES, (i + 1) * LANES)
        q_ref[:, at] = turn(both[:, at], cosine, sine).astype(bf16)
    kv_ref[:, :LANES] = turn(both[:, 3 * LANES : 4 * LANES], cosine, sine).astype(bf16)
    kv_ref[:, LANES:] = both[:, 4 * LANES :].astype(bf16)


def head_rows(values, j):
    pair = values[:, j // 2 * LANES : (j // 2 + 1) * LANES]
    if j % 2 != j // 3:
        pair = pltpu.roll(pair, HEAD, 1)
    low = iota(pair.shape, 1) < HEAD
    return jnp.where(low if j < 3 else jnp.logical_not(low), pair, 0.0)


def spread_heads(source_ref, target_ref, scale):
    rows = source_ref.shape[0]
    values = source_ref[...].astype(f32)
    for j in range(6):
        target_ref[j * rows : (j + 1) * rows, :] = (head_rows(values, j) * scale).astype(bf16)


def join_heads(wide, rows):
    heads = []
    for j in range(6):
        at = HEAD if j >= 3 else 0
        heads.append(wide[at : at + HEAD, j * rows : (j + 1) * rows])
    return [jnp.concatenate(heads[2 * p : 2 * p + 2], axis=0).T for p in range(3)]


def in_reach(row_ref, kb, rows, shape):
    ahead = iota((rows, shape[1]), 1) % rows - iota((rows, shape[1]), 0)
    count = shape[0] // rows
    parts = [ahead + (row_ref[0] - row_ref[1 + kb * count + i]) >= 0 for i in range(count)]
    return jnp.concatenate(parts, axis=0)


def attend_kernel(
    row_ref, wo_ref, q_ref, kv0, kv1, kv2, kv3, o_ref, l_ref, y_ref, qp, st
):
    rows = q_ref.shape[0]
    step = kv0.shape[0]
    spread_heads(q_ref, qp, 0.125)
    peak = None
    for kb, kv_ref in enumerate((kv0, kv1, kv2, kv3)):
        s = nt(kv_ref[:, :LANES], qp[...])
        s = jnp.where(in_reach(row_ref, kb, rows, s.shape), s, -1e30)
        st[kb * step : (kb + 1) * step, :] = s
        top = jnp.max(s, axis=0, keepdims=True)
        peak = top if peak is None else jnp.maximum(peak, top)
    total, wide = 0.0, 0.0
    for kb, kv_ref in enumerate((kv0, kv1, kv2, kv3)):
        p = jnp.exp(st[kb * step : (kb + 1) * step, :] - peak)
        total = total + jnp.sum(p, axis=0, keepdims=True)
        wide = wide + tn(kv_ref[:, LANES:], p.astype(bf16))
    wide = wide / total
    l_ref[...] = jnp.broadcast_to(peak + jnp.log(total), l_ref.shape)
    for p, part in enumerate(join_heads(wide, rows)):
        o_ref[:, p * LANES : (p + 1) * LANES] = part.astype(bf16)
    y_ref[...] = nn(o_ref[...], wo_ref[...]).astype(bf16)


def attend_back_kernel(
    row_ref, wo_ref, cos_ref, sin_ref, q_ref, kv0, kv1, kv2, kv3, da_ref, l_ref, o_ref,
    dq_ref, dkv0, dkv1, dkv2, dkv3, qp, dp, dob, prod,
):
    rows = q_ref.shape[0]
    spread_heads(q_ref, qp, 0.125)
    dob[...] = nt(da_ref[...], wo_ref[...]).astype(bf16)
    spread_heads(dob, dp, 1.0)
    both = dob[...].astype(f32) * o_ref[...].astype(f32)
    for j in range(6):
        prod[j * rows : (j + 1) * rows, :] = head_rows(both, j)
    inner = lax.dot_general(
        jnp.ones((8, LANES), f32),
        prod[...],
        (((1,), (1,)), ((), ())),
        precision=lax.Precision.HIGHEST,
        preferred_element_type=f32,
    )[0:1, :]
    log_total = l_ref[0:1, :]
    wide = 0.0
    for kb, (kv_ref, dkv_ref) in enumerate(((kv0, dkv0), (kv1, dkv1), (kv2, dkv2), (kv3, dkv3))):
        keys_here, values_here = kv_ref[:, :LANES], kv_ref[:, LANES:]
        s = nt(keys_here, qp[...])
        p = jnp.where(in_reach(row_ref, kb, rows, s.shape), jnp.exp(s - log_total), 0.0)
        ds = (p * (nt(values_here, dp[...]) - inner)).astype(bf16)
        dkv_ref[:, :LANES] = nn(ds, qp[...]).astype(bf16)
        dkv_ref[:, LANES:] = nn(p.astype(bf16), dp[...]).astype(bf16)
        wide = wide + tn(keys_here, ds)
    for p, part in enumerate(join_heads(wide * 0.125, rows)):
        dq_ref[:, p * LANES : (p + 1) * LANES] = turn(part, cos_ref[...], -sin_ref[...]).astype(bf16)


def after_keys_kernel(
    dkv0, dkv1, dkv2, dkv3, dq_ref, x_ref, w_ref, cos_ref, sin_ref, g_ref, y_ref, gain_ref
):
    whole = dkv0[...].astype(f32) + dkv1[...].astype(f32)
    whole = whole + (dkv2[...].astype(f32) + dkv3[...].astype(f32))
    g_ref[:, : 3 * LANES] = dq_ref[...]
    g_ref[:, 3 * LANES : 4 * LANES] = turn(whole[:, :LANES], cos_ref[...], -sin_ref[...]).astype(bf16)
    g_ref[:, 4 * LANES :] = whole[:, LANES:].astype(bf16)
    y = nt(g_ref[...], w_ref[...])
    y_ref[...] = y.astype(bf16)
    x = x_ref[...].astype(f32)
    root = lax.rsqrt(jnp.mean(x * x, axis=-1, keepdims=True) + epsilon)
    gain_ref[...] = jnp.broadcast_to(jnp.sum(y * (x * root), axis=0, keepdims=True), gain_ref.shape)


CHUNK = 256
HALF = CHUNK // GROUP * SLOTS


def picks(tgt_ref, ch):
    at = slice(ch * CHUNK, (ch + 1) * CHUNK)
    rows = iota((HALF, CHUNK), 0)
    return rows == tgt_ref[0:1, at], rows == tgt_ref[1:2, at]


def one_hot(pick_a, pick_b):
    return jnp.concatenate([pick_a.astype(f32), pick_b.astype(f32)], axis=0).astype(bf16)


def row_of(table, expert):
    return jnp.sum(jnp.where(iota(table.shape, 0) == expert, table, 0.0), axis=0, keepdims=True)


def two_of(refs, ch):
    return jnp.concatenate([refs[2 * ch][...], refs[2 * ch + 1][...]], axis=0)


def put_two(refs, ch, value):
    rows = value.shape[0] // 2
    refs[2 * ch][...] = value[:rows]
    refs[2 * ch + 1][...] = value[rows:]


def experts_kernel(s_ref, router, wg, wu, wd, *refs):
    tokens_in, refs = refs[: 2 * SIDE], refs[2 * SIDE :]
    tgt, mask, *refs = refs
    tokens_out, refs = refs[: 2 * SIDE], refs[2 * SIDE :]
    gates, slots_in, g_ref, u_ref, hidden, weights, scaled = refs
    chunks = SIDE
    for ch in range(chunks):
        at = slice(ch * CHUNK, (ch + 1) * CHUNK)
        z = nt(router[...], two_of(tokens_in, ch))
        chosen = mask[:, at]
        z = jnp.where(chosen > 0.0, z, -1e30)
        e = jnp.exp(z - jnp.max(z, axis=0, keepdims=True)) * chosen
        gates[:, at] = e / jnp.sum(e, axis=0, keepdims=True)
    rows = slots_in.shape[0] // 2
    for ch in range(chunks):
        pick_a, pick_b = picks(tgt, ch)
        got = nn(one_hot(pick_a, pick_b), two_of(tokens_in, ch)).astype(bf16)
        here = gates[:, ch * CHUNK : (ch + 1) * CHUNK]
        for which, pick in enumerate((pick_a, pick_b)):
            at = which * rows + ch * HALF
            slots_in[at : at + HALF, :] = got[which * HALF : (which + 1) * HALF]
            weight = jnp.sum(jnp.where(pick, row_of(here, s_ref[which]), 0.0), axis=1, keepdims=True)
            weights[at : at + HALF, :] = jnp.broadcast_to(weight, (HALF, LANES))
    hidden[...] = jnp.zeros_like(hidden)
    for k in range(wg.shape[1] // BLOCK):
        at = slice(k * BLOCK, (k + 1) * BLOCK)
        here = pl.ds(pl.multiple_of(s_ref[2 + k] * rows, rows), rows)
        both = nn(slots_in[here, :], jnp.concatenate([wg[:, at], wu[:, at]], axis=1))
        g, u = both[:, :BLOCK], both[:, BLOCK:]
        g_ref[:, at] = g
        u_ref[:, at] = u
        hidden[here, at] = (g * jax.nn.sigmoid(g) * u).astype(bf16)
    for at in range(0, wd.shape[1], CHUNK):
        part = nn(hidden[...], wd[:, at : at + CHUNK])
        scaled[:, at : at + CHUNK] = (part * weights[:, 0:1]).astype(bf16)
    for ch in range(chunks):
        at = ch * HALF
        both = jnp.concatenate([scaled[at : at + HALF], scaled[rows + at : rows + at + HALF]], axis=0)
        put_two(tokens_out, ch, tn(one_hot(*picks(tgt, ch)), both).astype(bf16))


def experts_back_kernel(s_ref, router, wg, wu, wd, *refs):
    grads_in, refs = refs[: 2 * SIDE], refs[2 * SIDE :]
    tgt, gates, g_ref, u_ref, *refs = refs
    grads_out, refs = refs[: 2 * SIDE], refs[2 * SIDE :]
    dgu_ref, h_ref, dy, dz_ref, inner, back = refs
    chunks = SIDE
    rows = dy.shape[0] // 2
    for ch in range(chunks):
        pick_a, pick_b = picks(tgt, ch)
        here = gates[:, ch * CHUNK : (ch + 1) * CHUNK]
        got = nn(one_hot(pick_a, pick_b), two_of(grads_in, ch))
        for which, pick in enumerate((pick_a, pick_b)):
            weight = jnp.sum(jnp.where(pick, row_of(here, s_ref[which]), 0.0), axis=1, keepdims=True)
            at = which * rows + ch * HALF
            dy[at : at + HALF, :] = (got[which * HALF : (which + 1) * HALF] * weight).astype(bf16)
    inner[...] = jnp.zeros_like(inner)
    back[...] = jnp.zeros_like(back)
    for k in range(wg.shape[1] // BLOCK):
        at = slice(k * BLOCK, (k + 1) * BLOCK)
        here = pl.ds(pl.multiple_of(s_ref[2 + k] * rows, rows), rows)
        dh = nt(dy[here, :], wd[at, :])
        g, u = g_ref[:, at], u_ref[:, at]
        sig = jax.nn.sigmoid(g)
        swish = g * sig
        h = (swish * u).astype(bf16)
        h_ref[:, at] = h
        inner[here, :] += jnp.broadcast_to(
            jnp.sum(h.astype(f32) * dh, axis=1, keepdims=True), (rows, LANES)
        )
        dg = (dh * u * sig * (1.0 + g * (1.0 - sig))).astype(bf16)
        du = (dh * swish).astype(bf16)
        both = jnp.concatenate([dg, du], axis=1)
        dgu_ref[:, 2 * k * BLOCK : 2 * (k + 1) * BLOCK] = both
        back[here, :] += nt(both, jnp.concatenate([wg[:, at], wu[:, at]], axis=1))
    for ch in range(chunks):
        pick_a, pick_b = picks(tgt, ch)
        span = slice(ch * CHUNK, (ch + 1) * CHUNK)
        sums = []
        for which, pick in enumerate((pick_a, pick_b)):
            at = which * rows + ch * HALF
            column = inner[at : at + HALF, 0:1]
            sums.append(jnp.sum(jnp.where(pick, column, 0.0), axis=0, keepdims=True))
        table = gates[:, span]
        expert = iota(table.shape, 0)
        dz = jnp.where(expert == s_ref[0], sums[0], 0.0) + jnp.where(expert == s_ref[1], sums[1], 0.0)
        dz = dz - table * (sums[0] + sums[1])
        high = dz.astype(bf16)
        lower = (dz - high.astype(f32)).astype(bf16)
        dz_ref[:, span] = jnp.concatenate([high, lower], axis=0)
        at = ch * HALF
        moved = jnp.concatenate([back[at : at + HALF, :], back[rows + at : rows + at + HALF, :]], axis=0)
        value = tn(
            jnp.concatenate([one_hot(pick_a, pick_b), high], axis=0),
            jnp.concatenate([moved.astype(bf16), router[...]], axis=0),
        )
        put_two(grads_out, ch, value.astype(bf16))


def router_kernel(dz_ref, *refs):
    tokens_in, (router_grad,) = refs[: 2 * SIDE], refs[2 * SIDE :]
    total = 0.0
    for ch in range(SIDE):
        total = total + nn(dz_ref[:, ch * CHUNK : (ch + 1) * CHUNK], two_of(tokens_in, ch))
    rows = router_grad.shape[0]
    total = total[:rows] + total[rows:]
    router_grad[...] = total + jnp.where(pl.program_id(0) == 0, 0.0, router_grad[...])


def expert_weights_kernel(
    s_ref, b_own, o0, o1, o2, h, dy, dgu, gate, up, near, far, down
):
    rows, size = h.shape[0], o1.shape[0]
    half = s_ref[2 + h.shape[1] // BLOCK]
    begin = pl.program_id(0) == 0
    for k in range(h.shape[1] // BLOCK):
        at = slice(k * BLOCK, (k + 1) * BLOCK)
        wide = slice(2 * k * BLOCK, 2 * (k + 1) * BLOCK)
        here = pl.ds(pl.multiple_of(s_ref[2 + k] * rows, rows), rows)
        first = s_ref[2 + k] == 0
        theirs = [jnp.where(first, o0[:size], o1[...]), jnp.where(first, o0[size:], o2[...])]
        both = tn(
            jnp.concatenate([b_own[here, :], *theirs], axis=0),
            jnp.concatenate([dgu[half, :, wide], dgu[1 - half, :, wide]], axis=0),
        )
        low = tn(h[:, at], dy[here, :])
        gate[:, at] = both[:, :BLOCK] + jnp.where(begin, 0.0, gate[:, at])
        up[:, at] = both[:, BLOCK:] + jnp.where(begin, 0.0, up[:, at])
        low = low + jnp.where(begin, 0.0, down[at, :])
        down[at, :] = low
        cut = at.start - near.shape[0]
        if cut < 0:
            near[at, :] = low.astype(bf16)
        else:
            far[cut : cut + BLOCK, :] = low.astype(bf16)


def ring(stage, steps):
    pairs = []
    for x in range(SIDE):
        for z in range(SIDE):
            for core in range(2):
                along_x = (core == 0) == (stage == 0)
                to = ((x + steps) % SIDE, z) if along_x else (x, (z + steps) % SIDE)
                pairs.append(((x * SIDE + z) * 2 + core, (to[0] * SIDE + to[1]) * 2 + core))
    return pairs


def other_core(value):
    return lax.ppermute(value, "ep", [(i, i ^ 1) for i in range(2 * CHIPS)])


def other_half(value):
    return lax.ppermute(value, "tp", [(0, 1), (1, 0)])


def other_both(value):
    pairs = [(2 * i + t, 2 * (i ^ 1) + 1 - t) for i in range(2 * CHIPS) for t in range(2)]
    return lax.ppermute(value, ("ep", "tp"), pairs)


def in_order(own, other, place, dim):
    return jnp.concatenate(
        [jnp.where(place == 0, own, other), jnp.where(place == 0, other, own)], axis=dim
    )


def from_ring(value, stage):
    return [value] + [lax.ppermute(value, "ep", ring(stage, -d)) for d in range(1, SIDE)]


def to_ring(pieces, stage):
    return [pieces[0]] + [
        lax.ppermute(pieces[d], "ep", ring(stage, d)) for d in range(1, SIDE)
    ]


def everyone(value):
    return from_ring(jnp.concatenate(from_ring(value, 0), axis=1), 1)


def added(pieces):
    pieces = [p.astype(f32) for p in pieces]
    return (pieces[0] + pieces[1]) + (pieces[2] + pieces[3])


def pieces_of(value):
    size = value.shape[1] // SIDE
    return [value[:, d * size : (d + 1) * size] for d in range(SIDE)]


def to_owners(pieces, beside=()):
    joined, *beside = pin(added(to_ring(pieces, 1)).astype(bf16), *beside)
    return to_ring(pieces_of(joined), 0), beside


def pin(*values):
    return lax.optimization_barrier(values)


SAME_CORE = [[2 * chip + core for chip in range(CHIPS)] for core in range(2)]


def exchange(pieces, groups=SAME_CORE):
    return lax.all_to_all(pieces, "ep", 0, 0, tiled=True, axis_index_groups=groups)


def broadcast(value, count=CHIPS, groups=SAME_CORE):
    return exchange(jnp.broadcast_to(value[None], (count, *value.shape)), groups)


def half_of(value, place, dim=0):
    size = value.shape[dim] // 2
    mine = lax.dynamic_slice_in_dim(value, place * size, size, dim)
    rest = lax.dynamic_slice_in_dim(value, (1 - place) * size, size, dim)
    return mine, rest


def body(
    x_in, cotangent, norm1_gain, wq, wk, wv, wo, norm2_gain, router, w_gate, w_up, w_down, routes
):
    section = lax.axis_index("section")
    rank = lax.axis_index("ep")
    half = lax.axis_index("tp")
    chip, core = rank // 2, rank % 2
    x, z = chip // SIDE, chip % SIDE
    micros, core_rows, width = x_in.shape
    own_rows = core_rows // 2
    chip_rows = core_rows * 2
    length = chip_rows * CHIPS
    experts = router.shape[2]
    blocks = w_gate.shape[2] // BLOCK
    gain_one = norm1_gain.reshape(1, width)
    gain_two = norm2_gain.reshape(1, width)
    gate_w, up_w, down_w = w_gate[0], w_up[0], w_down[0]
    expert_rows = -(-experts // 16) * 16
    router_t = jnp.pad(router[0].T, ((0, expert_rows - experts), (0, 0)))

    qkv_w = jnp.concatenate([half_of(w[0], core, 1)[0] for w in (wq, wk, wv)], axis=1)
    out_w = half_of(wo[0], core)[0]

    first_row = (chip * chip_rows).astype(jnp.int32)
    positions = (first_row + jnp.arange(chip_rows, dtype=jnp.int32)).astype(f32)
    quarter = HEAD // 2
    frequency = 10000.0 ** (-jnp.arange(quarter, dtype=f32) * 2.0 / HEAD)
    phase = positions[:, None] * frequency[None, :]
    cosine = jnp.tile(jnp.cos(phase), (1, 4))
    sine = jnp.concatenate([-jnp.sin(phase), jnp.sin(phase)] * 2, axis=1)

    def chips_met(which_core):
        inner, outer = jnp.arange(CHIPS) % SIDE, jnp.arange(CHIPS) // SIDE
        by_x = jnp.where(which_core == 0, inner, outer)
        by_z = jnp.where(which_core == 0, outer, inner)
        return ((x + by_x) % SIDE) * SIDE + (z + by_z) % SIDE

    row_scalars = jnp.concatenate(
        [first_row.reshape(1), chips_met(core) * chip_rows]
    ).astype(jnp.int32)

    first_expert = rank * blocks // EXPERT_BLOCKS
    which = (rank * blocks + jnp.arange(blocks)) // EXPERT_BLOCKS - first_expert
    scalars = jnp.concatenate(
        [jnp.stack([first_expert, first_expert + 1]), which, half.reshape(1)]
    ).astype(jnp.int32)

    tokens = CHIPS * own_rows
    slot_rows = 2 * 2 * CHIPS * SLOTS
    hidden_width = blocks * BLOCK
    both_rows = micros * chip_rows
    cosines, sines = jnp.tile(cosine, (micros, 1)), jnp.tile(sine, (micros, 1))

    def prepare(own_routes):
        all_routes = broadcast(own_routes.reshape(-1, LANES), 2 * CHIPS, None)
        met = jnp.concatenate([chips_met(core) * 2 + core, chips_met(1 - core) * 2 + 1 - core])
        all_routes = jnp.take(all_routes, met, axis=0)
        both_routes = all_routes.reshape(2 * CHIPS, micros, own_rows, TOPK).transpose(1, 0, 2, 3)
        both_routes = both_routes.reshape(micros, 2 * CHIPS * own_rows, TOPK)
        named = (
            both_routes[:, None, :, :] == jnp.arange(expert_rows, dtype=jnp.int32)[None, :, None, None]
        )
        masks = jnp.any(named, axis=-1).astype(f32)
        wanted = jnp.stack([first_expert, first_expert + 1]).astype(jnp.int32)
        hits = jnp.any(both_routes[:, None, :, :] == wanted[None, :, None, None], axis=-1)
        hits = hits.reshape(micros, 2, 2 * CHIPS, own_rows).astype(jnp.int32)
        before = jnp.cumsum(hits, axis=-1) - hits
        base = (jnp.arange(2 * CHIPS, dtype=jnp.int32) % (CHUNK // GROUP)) * SLOTS
        targets = jnp.where(hits > 0, base[None, None, :, None] + before, -1)
        targets = targets.reshape(micros, 2, 2 * CHIPS * own_rows)
        return targets, masks

    def project(x128):
        a, q, kv = local_call(
            project_kernel,
            [((both_rows, width), bf16), ((both_rows, 3 * LANES), bf16), ((both_rows, 2 * LANES), bf16)],
            [x128.reshape(both_rows, width), gain_one, qkv_w, cosines, sines],
            flops=2 * both_rows * width * 5 * LANES,
            vmem=16,
        )
        return a, q.reshape(micros, chip_rows, -1), kv.reshape(micros, chip_rows, -1)

    def attend(q, kv):
        return local_call(
            attend_kernel,
            [((chip_rows, 3 * LANES), bf16), ((8, 6 * chip_rows), f32), ((chip_rows, width), bf16)],
            [row_scalars, out_w],
            each=[q, *kv],
            scratch=[((6 * chip_rows, LANES), bf16), ((length, 6 * chip_rows), f32)],
            flops=8 * micros * length * 6 * chip_rows * LANES,
            smem=1,
            vmem=32,
            micros=micros,
        )

    def attend_back(q, kv, grad, log_total, o):
        return local_call(
            attend_back_kernel,
            [((chip_rows, 3 * LANES), bf16)] + [((length // SIDE, 2 * LANES), bf16)] * SIDE,
            [row_scalars, out_w, cosine, sine],
            each=[q, *kv, grad, log_total, o],
            scratch=[
                ((6 * chip_rows, LANES), bf16),
                ((6 * chip_rows, LANES), bf16),
                ((chip_rows, 3 * LANES), bf16),
                ((6 * chip_rows, LANES), f32),
            ],
            flops=20 * micros * length * 6 * chip_rows * LANES,
            smem=1,
            vmem=60,
            micros=micros,
        )

    def after_keys(arrived, dq, x128):
        dqkv, y, gain = local_call(
            after_keys_kernel,
            [((both_rows, 5 * LANES), bf16), ((both_rows, width), bf16), ((8, width), f32)],
            [v.reshape(both_rows, -1) for v in (*arrived, dq, x128)] + [qkv_w, cosines, sines],
            flops=2 * both_rows * width * 5 * LANES,
            vmem=16,
        )
        return dqkv, y.reshape(micros, chip_rows, width), gain[:1]

    piece = ((tokens // SIDE, width), bf16)

    def run_experts(arrived):
        result = local_call(
            experts_kernel,
            [piece] * (2 * SIDE)
            + [
                ((expert_rows, 2 * tokens), f32),
                ((slot_rows, width), bf16),
                ((slot_rows // 2, hidden_width), f32),
                ((slot_rows // 2, hidden_width), f32),
            ],
            [scalars, router_t, gate_w, up_w, down_w],
            each=[*arrived, targets, masks],
            scratch=[
                ((slot_rows, hidden_width), bf16),
                ((slot_rows, LANES), f32),
                ((slot_rows, width), bf16),
            ],
            flops=10 * micros * slot_rows * hidden_width * width,
            smem=1,
            vmem=48,
            micros=micros,
        )
        return result[: 2 * SIDE], result[2 * SIDE :]

    def run_experts_back(grads, gates, g, u):
        result = local_call(
            experts_back_kernel,
            [piece] * (2 * SIDE)
            + [
                ((slot_rows // 2, 2 * hidden_width), bf16),
                ((slot_rows // 2, hidden_width), bf16),
                ((slot_rows, width), bf16),
                ((2 * expert_rows, 2 * tokens), bf16),
            ],
            [scalars, router_t, gate_w, up_w, down_w],
            each=[*grads, targets, gates, g, u],
            scratch=[((slot_rows, LANES), f32), ((slot_rows, width), f32)],
            flops=10 * micros * slot_rows * hidden_width * width,
            smem=1,
            vmem=52,
            micros=micros,
        )
        return result[: 2 * SIDE], result[2 * SIDE :]

    def sum_four(part):
        mine, rest = half_of(part, core, 1)
        mine, rest = half_of(mine.astype(f32) + other_core(rest).astype(f32), half, 1)
        return mine + other_half(rest.astype(bf16)).astype(f32)

    def to_four(rows32):
        rows64 = in_order(rows32, other_half(rows32), half, 1)
        return in_order(rows64, other_core(rows64), core, 1)

    def over_cores(parts):
        return [
            (own.astype(f32) + other_core(other).astype(f32)).astype(bf16)
            for own, other in zip(parts[:SIDE], parts[SIDE:])
        ]

    def tokens_back(parts, beside=()):
        pieces, beside = to_owners(over_cores(parts), beside)
        return added(pieces), beside

    def inverse_root(values):
        return lax.rsqrt(jnp.mean(values * values, axis=-1, keepdims=True) + epsilon)

    def norm_back(values, root, gradient, gain):
        weighted = gradient * gain
        return root * weighted - values * root**3 * jnp.mean(weighted * values, axis=-1, keepdims=True)

    def forward(own, x128, sent=None):
        nonlocal targets, masks
        a, q, kv = project(x128)
        kv_all = everyone(kv)
        o, log_total, y = attend(q, kv_all)
        residual = own.astype(f32) + sum_four(y)
        mixed = (residual * inverse_root(residual) * gain_two).astype(bf16)
        if sent is not None:
            own_routes = lax.dynamic_slice_in_dim(routes[0], half * own_rows, own_rows, 1)
            targets, masks = prepare(pin(own_routes, kv_all[0])[0])
            mixed = jnp.where(section == 0, mixed, sent)
        arrived = everyone(mixed)
        if sent is not None:
            *arrived, targets, masks = pin(*arrived, targets, masks)
        arrived = arrived + [other_core(p) for p in arrived]
        parts, rest = run_experts(arrived)
        return parts, (own, x128, a, q, kv_all, o, log_total, residual, arrived, *rest)

    def backward(grad_rows, grads, kept, between=None):
        residual, _, gates, _, g, u = kept[7:]
        parts, rest = run_experts_back(grads, gates, g, u)
        if between is None:
            mixed_grad = tokens_back(parts)[0]
        else:
            parts = between(*between(*parts, finish=True), start=True)
            (router_grad,) = local_call(
                router_kernel,
                [],
                [],
                each=[rest[3], *kept[8]],
                sums=[((expert_rows, width), f32)],
                flops=4 * micros * expert_rows * 2 * tokens * width,
                vmem=20,
                micros=micros,
            )
            pieces = to_ring(over_cores(parts), 1)
            joined, router_grad = between(added(pieces).astype(bf16), router_grad, finish=True)
            rest = (*rest[:3], router_grad)
            mixed_grad = added(to_ring(pieces_of(joined), 0))
        root = inverse_root(residual)
        gain_two_grad = jnp.sum(mixed_grad * residual * root, axis=(0, 1))
        resid_grad = grad_rows.astype(f32) + norm_back(residual, root, mixed_grad, gain_two)
        return resid_grad, rest, gain_two_grad

    targets = masks = None
    own_x = lax.dynamic_slice_in_dim(x_in, half * own_rows, own_rows, 1)
    x128 = in_order(x_in, other_core(x_in), core, 1)
    parts, kept = forward(own_x, x128, cotangent)
    upper_grads = kept[8]
    out = (kept[7] + tokens_back(parts)[0]).astype(bf16)
    same = lax.ppermute(out, "section", [(0, 1)])
    rows64 = in_order(same, lax.ppermute(out, ("section", "tp"), [(0, 3), (1, 2)]), half, 1)
    whole = in_order(rows64, other_core(rows64), core, 1)
    last_parts, kept = forward(
        jnp.where(section == 0, own_x, same), jnp.where(section == 0, x128, whole)
    )
    own, x128, a, q, kv_all, o, log_total, residual = kept[:8]
    own, slots_in = own.astype(f32), kept[10]

    resid_grad, *_ = backward(cotangent, upper_grads, kept)
    low, *joined = pin(resid_grad.astype(bf16), *over_cores(last_parts))
    pieces = to_ring(joined, 1)
    out_grad, rows = pin(to_four(low), slots_in[:, : slot_rows // 2])
    other_slots = [other_half(rows)]
    dq, *dkv = attend_back(q, kv_all, out_grad, log_total, o)
    *dkv, joined = pin(*dkv, added(pieces).astype(bf16))
    dkv, _ = to_owners(dkv)
    *dkv, joined, other_slots[0] = pin(*dkv, joined, other_slots[0])
    pieces = to_ring(pieces_of(joined), 0)
    _, y, _ = after_keys(dkv, dq, x128)
    normed_grad, out = pin(sum_four(y), (residual + added(pieces)).astype(bf16))
    root = inverse_root(own)
    upper = (resid_grad + norm_back(own, root, normed_grad, gain_one)).astype(bf16)
    coming = lax.ppermute(upper, "section", [(1, 0)])
    coming, other_out = pin(jnp.where(section == 0, coming, cotangent), other_half(out))
    activations = in_order(out, other_out, half, 1)

    cuts = [0, slot_rows // 2, slot_rows * 3 // 4, slot_rows]

    def between(*values, finish=False, start=False):
        if finish:
            *values, other_slots[-1] = pin(*values, other_slots[-1])
        if start:
            at, end = cuts[len(other_slots) :][:2]
            *values, rows = pin(*values, slots_in[:, at:end])
            other_slots.append(other_half(rows))
        return values

    arrived = between(*everyone(coming), start=True)
    grads = arrived + [other_core(p) for p in arrived]
    resid_grad, (dgu, h, dy, router_grad), gain_two_grad = backward(coming, grads, kept, between)
    out_grad = to_four(resid_grad.astype(bf16))
    all_dgu = lax.all_gather(dgu, "tp")
    out_w_grad = tn(o.reshape(both_rows, -1), out_grad.reshape(both_rows, width)).astype(bf16)
    out_w_grad = exchange(out_w_grad.reshape(CHIPS, -1, width))
    dq, *dkv = attend_back(q, kv_all, out_grad, log_total, o)
    dq, out_w_grad = pin(dq, out_w_grad)
    out_w_grad = jnp.sum(out_w_grad.astype(f32), axis=0).astype(bf16)
    near_rows = 2 * BLOCK
    gate_grad, up_grad, near, far = local_call(
        expert_weights_kernel,
        [],
        [scalars],
        each=[slots_in, *other_slots, h, dy],
        pairs=[all_dgu],
        sums=[
            ((width, hidden_width), f32),
            ((width, hidden_width), f32),
            ((near_rows, width), bf16),
            ((hidden_width - near_rows, width), bf16),
        ],
        scratch=[((hidden_width, width), f32)],
        flops=10 * slot_rows * hidden_width * width,
        smem=1,
        vmem=56,
        micros=micros,
    )
    all_out = lax.all_gather(out_w_grad, "ep")
    q_grad = tn(a, dq.reshape(both_rows, -1)).astype(bf16)
    q_grad = exchange(q_grad.reshape(CHIPS, -1, 3 * LANES))
    arrived, (gate_grad, up_grad, near, far, q_grad) = to_owners(
        dkv, (gate_grad, up_grad, near, far, q_grad)
    )
    q_grad = jnp.sum(q_grad.astype(f32), axis=0).astype(bf16)
    dqkv, y, gain_one_grad = after_keys(arrived, dq, x128)
    near_down = other_half(near)

    kv_width = 2 * LANES
    small = jnp.concatenate([router_grad[:experts], gain_one_grad, gain_two_grad[None]], axis=0)
    small_count = small.size
    small_lines = -(-small_count // (CHIPS * kv_width))
    small = jnp.pad(small.reshape(-1), (0, CHIPS * small_lines * kv_width - small_count))
    small = small.reshape(CHIPS, small_lines, kv_width).astype(bf16)
    wide = tn(a, dqkv[:, 3 * LANES :]).astype(bf16).reshape(CHIPS, -1, kv_width)
    lines = wide.shape[1]
    wide, near_down, all_out = pin(jnp.concatenate([wide, small], axis=1), near_down, all_out)
    all_q = lax.all_gather(pin(q_grad, all_out)[0], "ep")
    far_down = other_half(pin(far, near_down)[0])
    wide, y, far_down = pin(exchange(wide), y, far_down)
    normed_grad = sum_four(y)
    wide, normed_grad, all_q = pin(
        broadcast(jnp.sum(wide.astype(f32), axis=0).astype(bf16)), normed_grad, all_q
    )
    input_grads = (resid_grad + norm_back(own, root, normed_grad, gain_one)).astype(bf16)
    down_grad = jnp.concatenate(
        [near.astype(f32) + near_down.astype(f32), far.astype(f32) + far_down.astype(f32)], axis=0
    )
    small = wide[:, lines:].reshape(-1)[:small_count].reshape(experts + 2, width)
    small = small.astype(f32) + other_core(small).astype(f32)
    small = small + other_half(small.astype(bf16)).astype(f32)
    wide = wide[:, :lines].reshape(width, kv_width)
    other_wide = other_core(wide)

    def both_cores(start, end):
        return in_order(wide[:, start:end], other_wide[:, start:end], core, 1).astype(f32)

    grad_k = both_cores(0, LANES)
    grad_v = both_cores(LANES, 2 * LANES)
    all_q = all_q.reshape(CHIPS, 2, -1, 3 * LANES)
    grad_q = jnp.concatenate(
        [all_q[:, c].reshape(width, -1) for c in range(2)], axis=1
    ).astype(f32)
    all_out = all_out.reshape(CHIPS, 2, -1, width)
    grad_out = jnp.concatenate(
        [all_out[:, c].reshape(-1, width) for c in range(2)], axis=0
    ).astype(f32)
    return (
        activations[None],
        input_grads[None],
        small[experts][None],
        grad_q[None],
        grad_k[None],
        grad_v[None],
        grad_out[None],
        small[experts + 1][None],
        small[:experts].T[None],
        gate_grad[None],
        up_grad[None],
        down_grad[None],
    )


def solution(mesh):
    ep = "ep"
    ep_tp = ("ep", "tp")
    placed = (
        P(None, ep, None),
        P(None, ep_tp, None),
        P("section", None),
        P("section", None, "tp"),
        P("section", None, "tp"),
        P("section", None, "tp"),
        P("section", "tp", None),
        P("section", None),
        P("section", None, None),
        P("section", None, ep),
        P("section", None, ep),
        P("section", ep, None),
        P("section", None, ep, None),
    )
    return jax.shard_map(
        body,
        mesh=mesh,
        in_specs=placed,
        out_specs=(
            P("section", None, ep, None),
            P("section", None, ep_tp, None),
            P("section", None),
            P("section", None, "tp"),
            P("section", None, "tp"),
            P("section", None, "tp"),
            P("section", "tp", None),
            P("section", None),
            P("section", None, None),
            P("section", None, ep),
            P("section", None, ep),
            P("section", ep, None),
        ),
        check_vma=False,
    )
```

```python
import jax
import jax.numpy as jnp
import numpy as np
from jax import lax
from jax.experimental import pallas as pl
from jax.experimental.pallas import tpu as pltpu
from jax.sharding import PartitionSpec as P

HEAD = 64
TOPK = 8
BLOCK = 128
EXPERT_BLOCKS = 4
SIDE = 4
CHIPS = SIDE * SIDE
LANES = 128
SLOTS = 8
GROUP = 32
epsilon = 1e-05
bf16 = jnp.bfloat16
f32 = jnp.float32


def nn(a, b):
    return lax.dot_general(a, b, (((1,), (0,)), ((), ())), preferred_element_type=f32)


def nt(a, b):
    return lax.dot_general(a, b, (((1,), (1,)), ((), ())), preferred_element_type=f32)


def tn(a, b):
    return lax.dot_general(a, b, (((0,), (0,)), ((), ())), preferred_element_type=f32)


def iota(shape, dim):
    return lax.broadcasted_iota(jnp.int32, shape, dim)


def whole_spec(shape, **more):
    return pl.BlockSpec(shape, lambda m: (0,) * len(shape), **more)


def micro_spec(shape):
    return pl.BlockSpec((None, *shape), lambda m: (m, *(0,) * len(shape)))


def pair_spec(shape):
    return pl.BlockSpec((shape[0], None, *shape[2:]), lambda m: (0, m, *(0,) * len(shape[2:])))


def local_call(
    kernel, outs, operands, scratch=(), flops=0, smem=0, vmem=40, each=(), pairs=(), sums=(), micros=1
):
    each, pairs = list(each), list(pairs)
    moved = sum(int(np.prod(v.shape)) * v.dtype.itemsize for v in [*operands, *each, *pairs])
    moved += sum(micros * int(np.prod(s)) * jnp.dtype(d).itemsize for s, d in outs)
    params = dict(
        scratch_shapes=[pltpu.VMEM(s, d) for s, d in scratch],
        compiler_params=pltpu.CompilerParams(vmem_limit_bytes=vmem * 1024 * 1024),
        cost_estimate=pl.CostEstimate(flops=flops, bytes_accessed=moved, transcendentals=0),
    )
    scalars = [pl.BlockSpec(memory_space=pltpu.SMEM)] * smem
    if not each:
        return pl.pallas_call(
            kernel,
            out_shape=[jax.ShapeDtypeStruct(s, d) for s, d in outs],
            in_specs=scalars + [pl.BlockSpec(memory_space=pltpu.VMEM)] * (len(operands) - smem),
            out_specs=[pl.BlockSpec(memory_space=pltpu.VMEM)] * len(outs),
            **params,
        )(*operands)
    return pl.pallas_call(
        kernel,
        grid=(micros,),
        out_shape=[jax.ShapeDtypeStruct((micros, *s), d) for s, d in outs]
        + [jax.ShapeDtypeStruct(s, d) for s, d in sums],
        in_specs=scalars
        + [whole_spec(v.shape, pipeline_mode=pl.Buffered(1)) for v in operands[smem:]]
        + [micro_spec(v.shape[1:]) for v in each]
        + [pair_spec(v.shape) for v in pairs],
        out_specs=[micro_spec(s) for s, d in outs] + [whole_spec(s) for s, d in sums],
        **params,
    )(*operands, *each, *pairs)


def turn(values, cosine, sine):
    lane = iota(values.shape, 1) % HEAD
    partner = jnp.where(
        lane < HEAD // 2,
        pltpu.roll(values, LANES - HEAD // 2, 1),
        pltpu.roll(values, HEAD // 2, 1),
    )
    return values * cosine + partner * sine


def project_kernel(x_ref, gain_ref, w_ref, cos_ref, sin_ref, a_ref, q_ref, kv_ref):
    x = x_ref[...].astype(f32)
    root = lax.rsqrt(jnp.mean(x * x, axis=-1, keepdims=True) + epsilon)
    a = (x * root * gain_ref[...]).astype(bf16)
    a_ref[...] = a
    both = nn(a, w_ref[...])
    cosine, sine = cos_ref[...], sin_ref[...]
    for i in range(3):
        at = slice(i * LANES, (i + 1) * LANES)
        q_ref[:, at] = turn(both[:, at], cosine, sine).astype(bf16)
    kv_ref[:, :LANES] = turn(both[:, 3 * LANES : 4 * LANES], cosine, sine).astype(bf16)
    kv_ref[:, LANES:] = both[:, 4 * LANES :].astype(bf16)


def head_rows(values, j):
    pair = values[:, j // 2 * LANES : (j // 2 + 1) * LANES]
    if j % 2 != j // 3:
        pair = pltpu.roll(pair, HEAD, 1)
    low = iota(pair.shape, 1) < HEAD
    return jnp.where(low if j < 3 else jnp.logical_not(low), pair, 0.0)


def spread_heads(source_ref, target_ref, scale):
    rows = source_ref.shape[0]
    values = source_ref[...].astype(f32)
    for j in range(6):
        target_ref[j * rows : (j + 1) * rows, :] = (head_rows(values, j) * scale).astype(bf16)


def join_heads(wide, rows):
    heads = []
    for j in range(6):
        at = HEAD if j >= 3 else 0
        heads.append(wide[at : at + HEAD, j * rows : (j + 1) * rows])
    return [jnp.concatenate(heads[2 * p : 2 * p + 2], axis=0).T for p in range(3)]


def in_reach(row_ref, kb, rows, shape):
    ahead = iota((rows, shape[1]), 1) % rows - iota((rows, shape[1]), 0)
    count = shape[0] // rows
    parts = [ahead + (row_ref[0] - row_ref[1 + kb * count + i]) >= 0 for i in range(count)]
    return jnp.concatenate(parts, axis=0)


def attend_kernel(
    row_ref, wo_ref, q_ref, kv0, kv1, kv2, kv3, o_ref, l_ref, y_ref, qp, st
):
    rows = q_ref.shape[0]
    step = kv0.shape[0]
    spread_heads(q_ref, qp, 0.125)
    peak = None
    for kb, kv_ref in enumerate((kv0, kv1, kv2, kv3)):
        s = nt(kv_ref[:, :LANES], qp[...])
        s = jnp.where(in_reach(row_ref, kb, rows, s.shape), s, -1e30)
        st[kb * step : (kb + 1) * step, :] = s
        top = jnp.max(s, axis=0, keepdims=True)
        peak = top if peak is None else jnp.maximum(peak, top)
    total, wide = 0.0, 0.0
    for kb, kv_ref in enumerate((kv0, kv1, kv2, kv3)):
        p = jnp.exp(st[kb * step : (kb + 1) * step, :] - peak)
        total = total + jnp.sum(p, axis=0, keepdims=True)
        wide = wide + tn(kv_ref[:, LANES:], p.astype(bf16))
    wide = wide / total
    l_ref[...] = jnp.broadcast_to(peak + jnp.log(total), l_ref.shape)
    for p, part in enumerate(join_heads(wide, rows)):
        o_ref[:, p * LANES : (p + 1) * LANES] = part.astype(bf16)
    y_ref[...] = nn(o_ref[...], wo_ref[...]).astype(bf16)


def attend_back_kernel(
    row_ref, wo_ref, cos_ref, sin_ref, q_ref, kv0, kv1, kv2, kv3, da_ref, l_ref, o_ref,
    dq_ref, dkv0, dkv1, dkv2, dkv3, qp, dp, dob, prod,
):
    rows = q_ref.shape[0]
    spread_heads(q_ref, qp, 0.125)
    dob[...] = nt(da_ref[...], wo_ref[...]).astype(bf16)
    spread_heads(dob, dp, 1.0)
    both = dob[...].astype(f32) * o_ref[...].astype(f32)
    for j in range(6):
        prod[j * rows : (j + 1) * rows, :] = head_rows(both, j)
    inner = lax.dot_general(
        jnp.ones((8, LANES), f32),
        prod[...],
        (((1,), (1,)), ((), ())),
        precision=lax.Precision.HIGHEST,
        preferred_element_type=f32,
    )[0:1, :]
    log_total = l_ref[0:1, :]
    wide = 0.0
    for kb, (kv_ref, dkv_ref) in enumerate(((kv0, dkv0), (kv1, dkv1), (kv2, dkv2), (kv3, dkv3))):
        keys_here, values_here = kv_ref[:, :LANES], kv_ref[:, LANES:]
        s = nt(keys_here, qp[...])
        p = jnp.where(in_reach(row_ref, kb, rows, s.shape), jnp.exp(s - log_total), 0.0)
        ds = (p * (nt(values_here, dp[...]) - inner)).astype(bf16)
        dkv_ref[:, :LANES] = nn(ds, qp[...]).astype(bf16)
        dkv_ref[:, LANES:] = nn(p.astype(bf16), dp[...]).astype(bf16)
        wide = wide + tn(keys_here, ds)
    for p, part in enumerate(join_heads(wide * 0.125, rows)):
        dq_ref[:, p * LANES : (p + 1) * LANES] = turn(part, cos_ref[...], -sin_ref[...]).astype(bf16)


def after_keys_kernel(
    dkv0, dkv1, dkv2, dkv3, dq_ref, x_ref, w_ref, cos_ref, sin_ref, g_ref, y_ref, gain_ref
):
    whole = dkv0[...].astype(f32) + dkv1[...].astype(f32)
    whole = whole + (dkv2[...].astype(f32) + dkv3[...].astype(f32))
    g_ref[:, : 3 * LANES] = dq_ref[...]
    g_ref[:, 3 * LANES : 4 * LANES] = turn(whole[:, :LANES], cos_ref[...], -sin_ref[...]).astype(bf16)
    g_ref[:, 4 * LANES :] = whole[:, LANES:].astype(bf16)
    y = nt(g_ref[...], w_ref[...])
    y_ref[...] = y.astype(bf16)
    x = x_ref[...].astype(f32)
    root = lax.rsqrt(jnp.mean(x * x, axis=-1, keepdims=True) + epsilon)
    gain_ref[...] = jnp.broadcast_to(jnp.sum(y * (x * root), axis=0, keepdims=True), gain_ref.shape)


CHUNK = 256
HALF = CHUNK // GROUP * SLOTS


def picks(tgt_ref, ch):
    at = slice(ch * CHUNK, (ch + 1) * CHUNK)
    rows = iota((HALF, CHUNK), 0)
    return rows == tgt_ref[0:1, at], rows == tgt_ref[1:2, at]


def one_hot(pick_a, pick_b):
    return jnp.concatenate([pick_a.astype(f32), pick_b.astype(f32)], axis=0).astype(bf16)


def row_of(table, expert):
    return jnp.sum(jnp.where(iota(table.shape, 0) == expert, table, 0.0), axis=0, keepdims=True)


def two_of(refs, ch):
    return jnp.concatenate([refs[2 * ch][...], refs[2 * ch + 1][...]], axis=0)


def put_two(refs, ch, value):
    rows = value.shape[0] // 2
    refs[2 * ch][...] = value[:rows]
    refs[2 * ch + 1][...] = value[rows:]


def experts_kernel(s_ref, router, wg, wu, wd, *refs):
    tokens_in, refs = refs[: 2 * SIDE], refs[2 * SIDE :]
    tgt, mask, *refs = refs
    tokens_out, refs = refs[: 2 * SIDE], refs[2 * SIDE :]
    gates, slots_in, g_ref, u_ref, hidden, weights, scaled = refs
    chunks = SIDE
    for ch in range(chunks):
        at = slice(ch * CHUNK, (ch + 1) * CHUNK)
        z = nt(router[...], two_of(tokens_in, ch))
        chosen = mask[:, at]
        z = jnp.where(chosen > 0.0, z, -1e30)
        e = jnp.exp(z - jnp.max(z, axis=0, keepdims=True)) * chosen
        gates[:, at] = e / jnp.sum(e, axis=0, keepdims=True)
    rows = slots_in.shape[0] // 2
    for ch in range(chunks):
        pick_a, pick_b = picks(tgt, ch)
        got = nn(one_hot(pick_a, pick_b), two_of(tokens_in, ch)).astype(bf16)
        here = gates[:, ch * CHUNK : (ch + 1) * CHUNK]
        for which, pick in enumerate((pick_a, pick_b)):
            at = which * rows + ch * HALF
            slots_in[at : at + HALF, :] = got[which * HALF : (which + 1) * HALF]
            weight = jnp.sum(jnp.where(pick, row_of(here, s_ref[which]), 0.0), axis=1, keepdims=True)
            weights[at : at + HALF, :] = jnp.broadcast_to(weight, (HALF, LANES))
    hidden[...] = jnp.zeros_like(hidden)
    for k in range(wg.shape[1] // BLOCK):
        at = slice(k * BLOCK, (k + 1) * BLOCK)
        here = pl.ds(pl.multiple_of(s_ref[2 + k] * rows, rows), rows)
        both = nn(slots_in[here, :], jnp.concatenate([wg[:, at], wu[:, at]], axis=1))
        g, u = both[:, :BLOCK], both[:, BLOCK:]
        g_ref[:, at] = g
        u_ref[:, at] = u
        hidden[here, at] = (g * jax.nn.sigmoid(g) * u).astype(bf16)
    for at in range(0, wd.shape[1], CHUNK):
        part = nn(hidden[...], wd[:, at : at + CHUNK])
        scaled[:, at : at + CHUNK] = (part * weights[:, 0:1]).astype(bf16)
    for ch in range(chunks):
        at = ch * HALF
        both = jnp.concatenate([scaled[at : at + HALF], scaled[rows + at : rows + at + HALF]], axis=0)
        put_two(tokens_out, ch, tn(one_hot(*picks(tgt, ch)), both).astype(bf16))


def experts_back_kernel(s_ref, router, wg, wu, wd, *refs):
    grads_in, refs = refs[: 2 * SIDE], refs[2 * SIDE :]
    tgt, gates, g_ref, u_ref, *refs = refs
    grads_out, refs = refs[: 2 * SIDE], refs[2 * SIDE :]
    dgu_ref, h_ref, dy, dz_ref, inner, back = refs
    chunks = SIDE
    rows = dy.shape[0] // 2
    for ch in range(chunks):
        pick_a, pick_b = picks(tgt, ch)
        here = gates[:, ch * CHUNK : (ch + 1) * CHUNK]
        got = nn(one_hot(pick_a, pick_b), two_of(grads_in, ch))
        for which, pick in enumerate((pick_a, pick_b)):
            weight = jnp.sum(jnp.where(pick, row_of(here, s_ref[which]), 0.0), axis=1, keepdims=True)
            at = which * rows + ch * HALF
            dy[at : at + HALF, :] = (got[which * HALF : (which + 1) * HALF] * weight).astype(bf16)
    inner[...] = jnp.zeros_like(inner)
    back[...] = jnp.zeros_like(back)
    for k in range(wg.shape[1] // BLOCK):
        at = slice(k * BLOCK, (k + 1) * BLOCK)
        here = pl.ds(pl.multiple_of(s_ref[2 + k] * rows, rows), rows)
        dh = nt(dy[here, :], wd[at, :])
        g, u = g_ref[:, at], u_ref[:, at]
        sig = jax.nn.sigmoid(g)
        swish = g * sig
        h = (swish * u).astype(bf16)
        h_ref[:, at] = h
        inner[here, :] += jnp.broadcast_to(
            jnp.sum(h.astype(f32) * dh, axis=1, keepdims=True), (rows, LANES)
        )
        dg = (dh * u * sig * (1.0 + g * (1.0 - sig))).astype(bf16)
        du = (dh * swish).astype(bf16)
        both = jnp.concatenate([dg, du], axis=1)
        dgu_ref[:, 2 * k * BLOCK : 2 * (k + 1) * BLOCK] = both
        back[here, :] += nt(both, jnp.concatenate([wg[:, at], wu[:, at]], axis=1))
    for ch in range(chunks):
        pick_a, pick_b = picks(tgt, ch)
        span = slice(ch * CHUNK, (ch + 1) * CHUNK)
        sums = []
        for which, pick in enumerate((pick_a, pick_b)):
            at = which * rows + ch * HALF
            column = inner[at : at + HALF, 0:1]
            sums.append(jnp.sum(jnp.where(pick, column, 0.0), axis=0, keepdims=True))
        table = gates[:, span]
        expert = iota(table.shape, 0)
        dz = jnp.where(expert == s_ref[0], sums[0], 0.0) + jnp.where(expert == s_ref[1], sums[1], 0.0)
        dz = dz - table * (sums[0] + sums[1])
        high = dz.astype(bf16)
        lower = (dz - high.astype(f32)).astype(bf16)
        dz_ref[:, span] = jnp.concatenate([high, lower], axis=0)
        at = ch * HALF
        moved = jnp.concatenate([back[at : at + HALF, :], back[rows + at : rows + at + HALF, :]], axis=0)
        value = tn(
            jnp.concatenate([one_hot(pick_a, pick_b), high], axis=0),
            jnp.concatenate([moved.astype(bf16), router[...]], axis=0),
        )
        put_two(grads_out, ch, value.astype(bf16))


def router_kernel(dz_ref, *refs):
    tokens_in, (router_grad,) = refs[: 2 * SIDE], refs[2 * SIDE :]
    total = 0.0
    for ch in range(SIDE):
        total = total + nn(dz_ref[:, ch * CHUNK : (ch + 1) * CHUNK], two_of(tokens_in, ch))
    rows = router_grad.shape[0]
    total = total[:rows] + total[rows:]
    router_grad[...] = total + jnp.where(pl.program_id(0) == 0, 0.0, router_grad[...])


def expert_weights_kernel(
    s_ref, b_own, o0, o1, o2, h, dy, dgu, gate, up, near, far, down
):
    rows, size = h.shape[0], o1.shape[0]
    half = s_ref[2 + h.shape[1] // BLOCK]
    begin = pl.program_id(0) == 0
    for k in range(h.shape[1] // BLOCK):
        at = slice(k * BLOCK, (k + 1) * BLOCK)
        wide = slice(2 * k * BLOCK, 2 * (k + 1) * BLOCK)
        here = pl.ds(pl.multiple_of(s_ref[2 + k] * rows, rows), rows)
        first = s_ref[2 + k] == 0
        theirs = [jnp.where(first, o0[:size], o1[...]), jnp.where(first, o0[size:], o2[...])]
        both = tn(
            jnp.concatenate([b_own[here, :], *theirs], axis=0),
            jnp.concatenate([dgu[half, :, wide], dgu[1 - half, :, wide]], axis=0),
        )
        low = tn(h[:, at], dy[here, :])
        gate[:, at] = both[:, :BLOCK] + jnp.where(begin, 0.0, gate[:, at])
        up[:, at] = both[:, BLOCK:] + jnp.where(begin, 0.0, up[:, at])
        low = low + jnp.where(begin, 0.0, down[at, :])
        down[at, :] = low
        cut = at.start - near.shape[0]
        if cut < 0:
            near[at, :] = low.astype(bf16)
        else:
            far[cut : cut + BLOCK, :] = low.astype(bf16)


def ring(stage, steps):
    pairs = []
    for x in range(SIDE):
        for z in range(SIDE):
            for core in range(2):
                along_x = (core == 0) == (stage == 0)
                to = ((x + steps) % SIDE, z) if along_x else (x, (z + steps) % SIDE)
                pairs.append(((x * SIDE + z) * 2 + core, (to[0] * SIDE + to[1]) * 2 + core))
    return pairs


def other_core(value):
    return lax.ppermute(value, "ep", [(i, i ^ 1) for i in range(2 * CHIPS)])


def other_half(value):
    return lax.ppermute(value, "tp", [(0, 1), (1, 0)])


def other_both(value):
    pairs = [(2 * i + t, 2 * (i ^ 1) + 1 - t) for i in range(2 * CHIPS) for t in range(2)]
    return lax.ppermute(value, ("ep", "tp"), pairs)


def in_order(own, other, place, dim):
    return jnp.concatenate(
        [jnp.where(place == 0, own, other), jnp.where(place == 0, other, own)], axis=dim
    )


def from_ring(value, stage):
    return [value] + [lax.ppermute(value, "ep", ring(stage, -d)) for d in range(1, SIDE)]


def to_ring(pieces, stage):
    return [pieces[0]] + [
        lax.ppermute(pieces[d], "ep", ring(stage, d)) for d in range(1, SIDE)
    ]


def everyone(value):
    return from_ring(jnp.concatenate(from_ring(value, 0), axis=1), 1)


def added(pieces):
    pieces = [p.astype(f32) for p in pieces]
    return (pieces[0] + pieces[1]) + (pieces[2] + pieces[3])


def pieces_of(value):
    size = value.shape[1] // SIDE
    return [value[:, d * size : (d + 1) * size] for d in range(SIDE)]


def to_owners(pieces, beside=()):
    joined, *beside = pin(added(to_ring(pieces, 1)).astype(bf16), *beside)
    return to_ring(pieces_of(joined), 0), beside


def pin(*values):
    return lax.optimization_barrier(values)


SAME_CORE = [[2 * chip + core for chip in range(CHIPS)] for core in range(2)]


def exchange(pieces, groups=SAME_CORE):
    return lax.all_to_all(pieces, "ep", 0, 0, tiled=True, axis_index_groups=groups)


def broadcast(value, count=CHIPS, groups=SAME_CORE):
    return exchange(jnp.broadcast_to(value[None], (count, *value.shape)), groups)


def half_of(value, place, dim=0):
    size = value.shape[dim] // 2
    mine = lax.dynamic_slice_in_dim(value, place * size, size, dim)
    rest = lax.dynamic_slice_in_dim(value, (1 - place) * size, size, dim)
    return mine, rest


def body(
    x_in, cotangent, norm1_gain, wq, wk, wv, wo, norm2_gain, router, w_gate, w_up, w_down, routes
):
    section = lax.axis_index("section")
    rank = lax.axis_index("ep")
    half = lax.axis_index("tp")
    chip, core = rank // 2, rank % 2
    x, z = chip // SIDE, chip % SIDE
    micros, core_rows, width = x_in.shape
    own_rows = core_rows // 2
    chip_rows = core_rows * 2
    length = chip_rows * CHIPS
    experts = router.shape[2]
    blocks = w_gate.shape[2] // BLOCK
    gain_one = norm1_gain.reshape(1, width)
    gain_two = norm2_gain.reshape(1, width)
    gate_w, up_w, down_w = w_gate[0], w_up[0], w_down[0]
    expert_rows = -(-experts // 16) * 16
    router_t = jnp.pad(router[0].T, ((0, expert_rows - experts), (0, 0)))

    qkv_w = jnp.concatenate([half_of(w[0], core, 1)[0] for w in (wq, wk, wv)], axis=1)
    out_w = half_of(wo[0], core)[0]

    first_row = (chip * chip_rows).astype(jnp.int32)
    positions = (first_row + jnp.arange(chip_rows, dtype=jnp.int32)).astype(f32)
    quarter = HEAD // 2
    frequency = 10000.0 ** (-jnp.arange(quarter, dtype=f32) * 2.0 / HEAD)
    phase = positions[:, None] * frequency[None, :]
    cosine = jnp.tile(jnp.cos(phase), (1, 4))
    sine = jnp.concatenate([-jnp.sin(phase), jnp.sin(phase)] * 2, axis=1)

    def chips_met(which_core):
        inner, outer = jnp.arange(CHIPS) % SIDE, jnp.arange(CHIPS) // SIDE
        by_x = jnp.where(which_core == 0, inner, outer)
        by_z = jnp.where(which_core == 0, outer, inner)
        return ((x + by_x) % SIDE) * SIDE + (z + by_z) % SIDE

    row_scalars = jnp.concatenate(
        [first_row.reshape(1), chips_met(core) * chip_rows]
    ).astype(jnp.int32)

    first_expert = rank * blocks // EXPERT_BLOCKS
    which = (rank * blocks + jnp.arange(blocks)) // EXPERT_BLOCKS - first_expert
    scalars = jnp.concatenate(
        [jnp.stack([first_expert, first_expert + 1]), which, half.reshape(1)]
    ).astype(jnp.int32)

    tokens = CHIPS * own_rows
    slot_rows = 2 * 2 * CHIPS * SLOTS
    hidden_width = blocks * BLOCK
    both_rows = micros * chip_rows
    cosines, sines = jnp.tile(cosine, (micros, 1)), jnp.tile(sine, (micros, 1))

    def prepare(own_routes):
        all_routes = broadcast(own_routes.reshape(-1, LANES), 2 * CHIPS, None)
        met = jnp.concatenate([chips_met(core) * 2 + core, chips_met(1 - core) * 2 + 1 - core])
        all_routes = jnp.take(all_routes, met, axis=0)
        both_routes = all_routes.reshape(2 * CHIPS, micros, own_rows, TOPK).transpose(1, 0, 2, 3)
        both_routes = both_routes.reshape(micros, 2 * CHIPS * own_rows, TOPK)
        named = (
            both_routes[:, None, :, :] == jnp.arange(expert_rows, dtype=jnp.int32)[None, :, None, None]
        )
        masks = jnp.any(named, axis=-1).astype(f32)
        wanted = jnp.stack([first_expert, first_expert + 1]).astype(jnp.int32)
        hits = jnp.any(both_routes[:, None, :, :] == wanted[None, :, None, None], axis=-1)
        hits = hits.reshape(micros, 2, 2 * CHIPS, own_rows).astype(jnp.int32)
        before = jnp.cumsum(hits, axis=-1) - hits
        base = (jnp.arange(2 * CHIPS, dtype=jnp.int32) % (CHUNK // GROUP)) * SLOTS
        targets = jnp.where(hits > 0, base[None, None, :, None] + before, -1)
        targets = targets.reshape(micros, 2, 2 * CHIPS * own_rows)
        return targets, masks

    def project(x128):
        a, q, kv = local_call(
            project_kernel,
            [((both_rows, width), bf16), ((both_rows, 3 * LANES), bf16), ((both_rows, 2 * LANES), bf16)],
            [x128.reshape(both_rows, width), gain_one, qkv_w, cosines, sines],
            flops=2 * both_rows * width * 5 * LANES,
            vmem=16,
        )
        return a, q.reshape(micros, chip_rows, -1), kv.reshape(micros, chip_rows, -1)

    def attend(q, kv):
        return local_call(
            attend_kernel,
            [((chip_rows, 3 * LANES), bf16), ((8, 6 * chip_rows), f32), ((chip_rows, width), bf16)],
            [row_scalars, out_w],
            each=[q, *kv],
            scratch=[((6 * chip_rows, LANES), bf16), ((length, 6 * chip_rows), f32)],
            flops=8 * micros * length * 6 * chip_rows * LANES,
            smem=1,
            vmem=32,
            micros=micros,
        )

    def attend_back(q, kv, grad, log_total, o):
        return local_call(
            attend_back_kernel,
            [((chip_rows, 3 * LANES), bf16)] + [((length // SIDE, 2 * LANES), bf16)] * SIDE,
            [row_scalars, out_w, cosine, sine],
            each=[q, *kv, grad, log_total, o],
            scratch=[
                ((6 * chip_rows, LANES), bf16),
                ((6 * chip_rows, LANES), bf16),
                ((chip_rows, 3 * LANES), bf16),
                ((6 * chip_rows, LANES), f32),
            ],
            flops=20 * micros * length * 6 * chip_rows * LANES,
            smem=1,
            vmem=60,
            micros=micros,
        )

    def after_keys(arrived, dq, x128):
        dqkv, y, gain = local_call(
            after_keys_kernel,
            [((both_rows, 5 * LANES), bf16), ((both_rows, width), bf16), ((8, width), f32)],
            [v.reshape(both_rows, -1) for v in (*arrived, dq, x128)] + [qkv_w, cosines, sines],
            flops=2 * both_rows * width * 5 * LANES,
            vmem=16,
        )
        return dqkv, y.reshape(micros, chip_rows, width), gain[:1]

    piece = ((tokens // SIDE, width), bf16)

    def run_experts(arrived):
        result = local_call(
            experts_kernel,
            [piece] * (2 * SIDE)
            + [
                ((expert_rows, 2 * tokens), f32),
                ((slot_rows, width), bf16),
                ((slot_rows // 2, hidden_width), f32),
                ((slot_rows // 2, hidden_width), f32),
            ],
            [scalars, router_t, gate_w, up_w, down_w],
            each=[*arrived, targets, masks],
            scratch=[
                ((slot_rows, hidden_width), bf16),
                ((slot_rows, LANES), f32),
                ((slot_rows, width), bf16),
            ],
            flops=10 * micros * slot_rows * hidden_width * width,
            smem=1,
            vmem=48,
            micros=micros,
        )
        return result[: 2 * SIDE], result[2 * SIDE :]

    def run_experts_back(grads, gates, g, u):
        result = local_call(
            experts_back_kernel,
            [piece] * (2 * SIDE)
            + [
                ((slot_rows // 2, 2 * hidden_width), bf16),
                ((slot_rows // 2, hidden_width), bf16),
                ((slot_rows, width), bf16),
                ((2 * expert_rows, 2 * tokens), bf16),
            ],
            [scalars, router_t, gate_w, up_w, down_w],
            each=[*grads, targets, gates, g, u],
            scratch=[((slot_rows, LANES), f32), ((slot_rows, width), f32)],
            flops=10 * micros * slot_rows * hidden_width * width,
            smem=1,
            vmem=52,
            micros=micros,
        )
        return result[: 2 * SIDE], result[2 * SIDE :]

    def sum_four(part):
        mine, rest = half_of(part, core, 1)
        mine, rest = half_of(mine.astype(f32) + other_core(rest).astype(f32), half, 1)
        return mine + other_half(rest.astype(bf16)).astype(f32)

    def to_four(rows32):
        rows64 = in_order(rows32, other_half(rows32), half, 1)
        return in_order(rows64, other_core(rows64), core, 1)

    def over_cores(parts):
        return [
            (own.astype(f32) + other_core(other).astype(f32)).astype(bf16)
            for own, other in zip(parts[:SIDE], parts[SIDE:])
        ]

    def tokens_back(parts, beside=()):
        pieces, beside = to_owners(over_cores(parts), beside)
        return added(pieces), beside

    def inverse_root(values):
        return lax.rsqrt(jnp.mean(values * values, axis=-1, keepdims=True) + epsilon)

    def norm_back(values, root, gradient, gain):
        weighted = gradient * gain
        return root * weighted - values * root**3 * jnp.mean(weighted * values, axis=-1, keepdims=True)

    def forward(own, x128, sent=None):
        nonlocal targets, masks
        a, q, kv = project(x128)
        kv_all = everyone(kv)
        o, log_total, y = attend(q, kv_all)
        residual = own.astype(f32) + sum_four(y)
        mixed = (residual * inverse_root(residual) * gain_two).astype(bf16)
        if sent is not None:
            own_routes = lax.dynamic_slice_in_dim(routes[0], half * own_rows, own_rows, 1)
            targets, masks = prepare(pin(own_routes, kv_all[0])[0])
            mixed = jnp.where(section == 0, mixed, sent)
        arrived = everyone(mixed)
        if sent is not None:
            *arrived, targets, masks = pin(*arrived, targets, masks)
        arrived = arrived + [other_core(p) for p in arrived]
        parts, rest = run_experts(arrived)
        return parts, (own, x128, a, q, kv_all, o, log_total, residual, arrived, *rest)

    def backward(grad_rows, grads, kept, between=None):
        residual, _, gates, _, g, u = kept[7:]
        parts, rest = run_experts_back(grads, gates, g, u)
        if between is None:
            mixed_grad = tokens_back(parts)[0]
        else:
            parts = between(*between(*parts, finish=True), start=True)
            (router_grad,) = local_call(
                router_kernel,
                [],
                [],
                each=[rest[3], *kept[8]],
                sums=[((expert_rows, width), f32)],
                flops=4 * micros * expert_rows * 2 * tokens * width,
                vmem=20,
                micros=micros,
            )
            pieces = to_ring(over_cores(parts), 1)
            joined, router_grad = between(added(pieces).astype(bf16), router_grad, finish=True)
            rest = (*rest[:3], router_grad)
            mixed_grad = added(to_ring(pieces_of(joined), 0))
        root = inverse_root(residual)
        gain_two_grad = jnp.sum(mixed_grad * residual * root, axis=(0, 1))
        resid_grad = grad_rows.astype(f32) + norm_back(residual, root, mixed_grad, gain_two)
        return resid_grad, rest, gain_two_grad

    targets = masks = None
    own_x = lax.dynamic_slice_in_dim(x_in, half * own_rows, own_rows, 1)
    x128 = in_order(x_in, other_core(x_in), core, 1)
    parts, kept = forward(own_x, x128, cotangent)
    upper_grads = kept[8]
    out = (kept[7] + tokens_back(parts)[0]).astype(bf16)
    same = lax.ppermute(out, "section", [(0, 1)])
    rows64 = in_order(same, lax.ppermute(out, ("section", "tp"), [(0, 3), (1, 2)]), half, 1)
    whole = in_order(rows64, other_core(rows64), core, 1)
    last_parts, kept = forward(
        jnp.where(section == 0, own_x, same), jnp.where(section == 0, x128, whole)
    )
    own, x128, a, q, kv_all, o, log_total, residual = kept[:8]
    own, slots_in = own.astype(f32), kept[10]

    resid_grad, *_ = backward(cotangent, upper_grads, kept)
    low, *joined = pin(resid_grad.astype(bf16), *over_cores(last_parts))
    pieces = to_ring(joined, 1)
    out_grad, rows = pin(to_four(low), slots_in[:, : slot_rows // 2])
    other_slots = [other_half(rows)]
    dq, *dkv = attend_back(q, kv_all, out_grad, log_total, o)
    *dkv, joined = pin(*dkv, added(pieces).astype(bf16))
    dkv, _ = to_owners(dkv)
    *dkv, joined, other_slots[0] = pin(*dkv, joined, other_slots[0])
    pieces = to_ring(pieces_of(joined), 0)
    _, y, _ = after_keys(dkv, dq, x128)
    normed_grad, out = pin(sum_four(y), (residual + added(pieces)).astype(bf16))
    root = inverse_root(own)
    upper = (resid_grad + norm_back(own, root, normed_grad, gain_one)).astype(bf16)
    coming = lax.ppermute(upper, "section", [(1, 0)])
    coming, other_out = pin(jnp.where(section == 0, coming, cotangent), other_half(out))
    activations = in_order(out, other_out, half, 1)

    cuts = [0, slot_rows // 2, slot_rows * 3 // 4, slot_rows]

    def between(*values, finish=False, start=False):
        if finish:
            *values, other_slots[-1] = pin(*values, other_slots[-1])
        if start:
            at, end = cuts[len(other_slots) :][:2]
            *values, rows = pin(*values, slots_in[:, at:end])
            other_slots.append(other_half(rows))
        return values

    arrived = between(*everyone(coming), start=True)
    grads = arrived + [other_core(p) for p in arrived]
    resid_grad, (dgu, h, dy, router_grad), gain_two_grad = backward(coming, grads, kept, between)
    out_grad = to_four(resid_grad.astype(bf16))
    all_dgu = lax.all_gather(dgu, "tp")
    out_w_grad = tn(o.reshape(both_rows, -1), out_grad.reshape(both_rows, width)).astype(bf16)
    out_w_grad = exchange(out_w_grad.reshape(CHIPS, -1, width))
    dq, *dkv = attend_back(q, kv_all, out_grad, log_total, o)
    dq, out_w_grad, h = pin(dq, out_w_grad, h)
    out_w_grad = jnp.sum(out_w_grad.astype(f32), axis=0).astype(bf16)
    near_rows = 2 * BLOCK
    gate_grad, up_grad, near, far = local_call(
        expert_weights_kernel,
        [],
        [scalars],
        each=[slots_in, *other_slots, h, dy],
        pairs=[all_dgu],
        sums=[
            ((width, hidden_width), f32),
            ((width, hidden_width), f32),
            ((near_rows, width), bf16),
            ((hidden_width - near_rows, width), bf16),
        ],
        scratch=[((hidden_width, width), f32)],
        flops=10 * slot_rows * hidden_width * width,
        smem=1,
        vmem=56,
        micros=micros,
    )
    all_out = lax.all_gather(out_w_grad, "ep")
    near_down = other_half(near)
    arrived, (gate_grad, up_grad, late_dq) = to_owners(dkv, (gate_grad, up_grad, dq))
    q_grad = tn(a, late_dq.reshape(both_rows, -1)).astype(bf16)
    q_grad = exchange(q_grad.reshape(CHIPS, -1, 3 * LANES))
    *arrived, near_down = pin(*arrived, near_down)
    dqkv, y, gain_one_grad = after_keys(arrived, dq, x128)

    kv_width = 2 * LANES
    small = jnp.concatenate([router_grad[:experts], gain_one_grad, gain_two_grad[None]], axis=0)
    small_count = small.size
    small_lines = -(-small_count // (CHIPS * kv_width))
    small = jnp.pad(small.reshape(-1), (0, CHIPS * small_lines * kv_width - small_count))
    small = small.reshape(CHIPS, small_lines, kv_width).astype(bf16)
    wide = tn(a, dqkv[:, 3 * LANES :]).astype(bf16).reshape(CHIPS, -1, kv_width)
    lines = wide.shape[1]
    far_down = other_half(pin(far, near_down)[0])
    wide, y, far_down, all_out, q_grad = pin(
        exchange(jnp.concatenate([wide, small], axis=1)), y, far_down, all_out, q_grad
    )
    wide = jnp.sum(wide.astype(f32), axis=0).astype(bf16)
    q_grad = jnp.sum(q_grad.astype(f32), axis=0).astype(bf16)
    all_width = 5 * LANES
    per_chip = small_lines * kv_width
    small = wide[lines:].reshape(-1, LANES)
    small = jnp.pad(small, ((0, -small.shape[0] % 5), (0, 0))).reshape(-1, all_width)
    wide = jnp.concatenate(
        [jnp.concatenate([q_grad, wide[:lines]], axis=1), small], axis=0
    )
    normed_grad = sum_four(y)
    wide, normed_grad = pin(broadcast(wide), normed_grad)
    input_grads = (resid_grad + norm_back(own, root, normed_grad, gain_one)).astype(bf16)
    down_grad = jnp.concatenate(
        [near.astype(f32) + near_down.astype(f32), far.astype(f32) + far_down.astype(f32)], axis=0
    )
    small = wide[:, lines:].reshape(CHIPS, -1)[:, :per_chip].reshape(-1)[:small_count]
    small = small.reshape(experts + 2, width)
    small = small.astype(f32) + other_core(small).astype(f32)
    small = small + other_half(small.astype(bf16)).astype(f32)
    wide = wide[:, :lines].reshape(width, all_width)
    other_wide = other_core(wide)

    def both_cores(start, end):
        return in_order(wide[:, start:end], other_wide[:, start:end], core, 1).astype(f32)

    grad_q = both_cores(0, 3 * LANES)
    grad_k = both_cores(3 * LANES, 4 * LANES)
    grad_v = both_cores(4 * LANES, 5 * LANES)
    all_out = all_out.reshape(CHIPS, 2, -1, width)
    grad_out = jnp.concatenate(
        [all_out[:, c].reshape(-1, width) for c in range(2)], axis=0
    ).astype(f32)
    return (
        activations[None],
        input_grads[None],
        small[experts][None],
        grad_q[None],
        grad_k[None],
        grad_v[None],
        grad_out[None],
        small[experts + 1][None],
        small[:experts].T[None],
        gate_grad[None],
        up_grad[None],
        down_grad[None],
    )


def solution(mesh):
    ep = "ep"
    ep_tp = ("ep", "tp")
    placed = (
        P(None, ep, None),
        P(None, ep_tp, None),
        P("section", None),
        P("section", None, "tp"),
        P("section", None, "tp"),
        P("section", None, "tp"),
        P("section", "tp", None),
        P("section", None),
        P("section", None, None),
        P("section", None, ep),
        P("section", None, ep),
        P("section", ep, None),
        P("section", None, ep, None),
    )
    return jax.shard_map(
        body,
        mesh=mesh,
        in_specs=placed,
        out_specs=(
            P("section", None, ep, None),
            P("section", None, ep_tp, None),
            P("section", None),
            P("section", None, "tp"),
            P("section", None, "tp"),
            P("section", None, "tp"),
            P("section", "tp", None),
            P("section", None),
            P("section", None, None),
            P("section", None, ep),
            P("section", None, ep),
            P("section", ep, None),
        ),
        check_vma=False,
    )
```

```python
import jax
import jax.numpy as jnp
import numpy as np
from jax import lax
from jax.experimental import pallas as pl
from jax.experimental.pallas import tpu as pltpu
from jax.sharding import PartitionSpec as P

HEAD = 64
TOPK = 8
BLOCK = 128
EXPERT_BLOCKS = 4
SIDE = 4
CHIPS = SIDE * SIDE
LANES = 128
SLOTS = 8
GROUP = 32
epsilon = 1e-05
bf16 = jnp.bfloat16
f32 = jnp.float32


def nn(a, b):
    return lax.dot_general(a, b, (((1,), (0,)), ((), ())), preferred_element_type=f32)


def nt(a, b):
    return lax.dot_general(a, b, (((1,), (1,)), ((), ())), preferred_element_type=f32)


def tn(a, b):
    return lax.dot_general(a, b, (((0,), (0,)), ((), ())), preferred_element_type=f32)


def iota(shape, dim):
    return lax.broadcasted_iota(jnp.int32, shape, dim)


def whole_spec(shape, **more):
    return pl.BlockSpec(shape, lambda m: (0,) * len(shape), **more)


def micro_spec(shape):
    return pl.BlockSpec((None, *shape), lambda m: (m, *(0,) * len(shape)))


def pair_spec(shape):
    return pl.BlockSpec((shape[0], None, *shape[2:]), lambda m: (0, m, *(0,) * len(shape[2:])))


def local_call(
    kernel, outs, operands, scratch=(), flops=0, smem=0, vmem=40, each=(), pairs=(), sums=(), micros=1
):
    each, pairs = list(each), list(pairs)
    moved = sum(int(np.prod(v.shape)) * v.dtype.itemsize for v in [*operands, *each, *pairs])
    moved += sum(micros * int(np.prod(s)) * jnp.dtype(d).itemsize for s, d in outs)
    params = dict(
        scratch_shapes=[pltpu.VMEM(s, d) for s, d in scratch],
        compiler_params=pltpu.CompilerParams(vmem_limit_bytes=vmem * 1024 * 1024),
        cost_estimate=pl.CostEstimate(flops=flops, bytes_accessed=moved, transcendentals=0),
    )
    scalars = [pl.BlockSpec(memory_space=pltpu.SMEM)] * smem
    if not each:
        return pl.pallas_call(
            kernel,
            out_shape=[jax.ShapeDtypeStruct(s, d) for s, d in outs],
            in_specs=scalars + [pl.BlockSpec(memory_space=pltpu.VMEM)] * (len(operands) - smem),
            out_specs=[pl.BlockSpec(memory_space=pltpu.VMEM)] * len(outs),
            **params,
        )(*operands)
    return pl.pallas_call(
        kernel,
        grid=(micros,),
        out_shape=[jax.ShapeDtypeStruct((micros, *s), d) for s, d in outs]
        + [jax.ShapeDtypeStruct(s, d) for s, d in sums],
        in_specs=scalars
        + [whole_spec(v.shape, pipeline_mode=pl.Buffered(1)) for v in operands[smem:]]
        + [micro_spec(v.shape[1:]) for v in each]
        + [pair_spec(v.shape) for v in pairs],
        out_specs=[micro_spec(s) for s, d in outs] + [whole_spec(s) for s, d in sums],
        **params,
    )(*operands, *each, *pairs)


def turn(values, cosine, sine):
    lane = iota(values.shape, 1) % HEAD
    partner = jnp.where(
        lane < HEAD // 2,
        pltpu.roll(values, LANES - HEAD // 2, 1),
        pltpu.roll(values, HEAD // 2, 1),
    )
    return values * cosine + partner * sine


def project_kernel(x_ref, gain_ref, w_ref, cos_ref, sin_ref, a_ref, q_ref, kv_ref):
    x = x_ref[...].astype(f32)
    root = lax.rsqrt(jnp.mean(x * x, axis=-1, keepdims=True) + epsilon)
    a = (x * root * gain_ref[...]).astype(bf16)
    a_ref[...] = a
    both = nn(a, w_ref[...])
    cosine, sine = cos_ref[...], sin_ref[...]
    for i in range(3):
        at = slice(i * LANES, (i + 1) * LANES)
        q_ref[:, at] = turn(both[:, at], cosine, sine).astype(bf16)
    kv_ref[:, :LANES] = turn(both[:, 3 * LANES : 4 * LANES], cosine, sine).astype(bf16)
    kv_ref[:, LANES:] = both[:, 4 * LANES :].astype(bf16)


def head_rows(values, j):
    pair = values[:, j // 2 * LANES : (j // 2 + 1) * LANES]
    if j % 2 != j // 3:
        pair = pltpu.roll(pair, HEAD, 1)
    low = iota(pair.shape, 1) < HEAD
    return jnp.where(low if j < 3 else jnp.logical_not(low), pair, 0.0)


def spread_heads(source_ref, target_ref, scale):
    rows = source_ref.shape[0]
    values = source_ref[...].astype(f32)
    for j in range(6):
        target_ref[j * rows : (j + 1) * rows, :] = (head_rows(values, j) * scale).astype(bf16)


def join_heads(wide, rows):
    heads = []
    for j in range(6):
        at = HEAD if j >= 3 else 0
        heads.append(wide[at : at + HEAD, j * rows : (j + 1) * rows])
    return [jnp.concatenate(heads[2 * p : 2 * p + 2], axis=0).T for p in range(3)]


def in_reach(row_ref, kb, rows, shape):
    ahead = iota((rows, shape[1]), 1) % rows - iota((rows, shape[1]), 0)
    count = shape[0] // rows
    parts = [ahead + (row_ref[0] - row_ref[1 + kb * count + i]) >= 0 for i in range(count)]
    return jnp.concatenate(parts, axis=0)


def attend_kernel(
    row_ref, wo_ref, q_ref, kv0, kv1, kv2, kv3, o_ref, l_ref, y_ref, qp, st
):
    rows = q_ref.shape[0]
    step = kv0.shape[0]
    spread_heads(q_ref, qp, 0.125)
    peak = None
    for kb, kv_ref in enumerate((kv0, kv1, kv2, kv3)):
        s = nt(kv_ref[:, :LANES], qp[...])
        s = jnp.where(in_reach(row_ref, kb, rows, s.shape), s, -1e30)
        st[kb * step : (kb + 1) * step, :] = s
        top = jnp.max(s, axis=0, keepdims=True)
        peak = top if peak is None else jnp.maximum(peak, top)
    total, wide = 0.0, 0.0
    for kb, kv_ref in enumerate((kv0, kv1, kv2, kv3)):
        p = jnp.exp(st[kb * step : (kb + 1) * step, :] - peak)
        total = total + jnp.sum(p, axis=0, keepdims=True)
        wide = wide + tn(kv_ref[:, LANES:], p.astype(bf16))
    wide = wide / total
    l_ref[...] = jnp.broadcast_to(peak + jnp.log(total), l_ref.shape)
    for p, part in enumerate(join_heads(wide, rows)):
        o_ref[:, p * LANES : (p + 1) * LANES] = part.astype(bf16)
    y_ref[...] = nn(o_ref[...], wo_ref[...]).astype(bf16)


def attend_back_kernel(
    row_ref, wo_ref, cos_ref, sin_ref, q_ref, kv0, kv1, kv2, kv3, da_ref, l_ref, o_ref,
    dq_ref, dkv0, dkv1, dkv2, dkv3, qp, dp, dob, prod,
):
    rows = q_ref.shape[0]
    spread_heads(q_ref, qp, 0.125)
    dob[...] = nt(da_ref[...], wo_ref[...]).astype(bf16)
    spread_heads(dob, dp, 1.0)
    both = dob[...].astype(f32) * o_ref[...].astype(f32)
    for j in range(6):
        prod[j * rows : (j + 1) * rows, :] = head_rows(both, j)
    inner = lax.dot_general(
        jnp.ones((8, LANES), f32),
        prod[...],
        (((1,), (1,)), ((), ())),
        precision=lax.Precision.HIGHEST,
        preferred_element_type=f32,
    )[0:1, :]
    log_total = l_ref[0:1, :]
    wide = 0.0
    for kb, (kv_ref, dkv_ref) in enumerate(((kv0, dkv0), (kv1, dkv1), (kv2, dkv2), (kv3, dkv3))):
        keys_here, values_here = kv_ref[:, :LANES], kv_ref[:, LANES:]
        s = nt(keys_here, qp[...])
        p = jnp.where(in_reach(row_ref, kb, rows, s.shape), jnp.exp(s - log_total), 0.0)
        ds = (p * (nt(values_here, dp[...]) - inner)).astype(bf16)
        dkv_ref[:, :LANES] = nn(ds, qp[...]).astype(bf16)
        dkv_ref[:, LANES:] = nn(p.astype(bf16), dp[...]).astype(bf16)
        wide = wide + tn(keys_here, ds)
    for p, part in enumerate(join_heads(wide * 0.125, rows)):
        dq_ref[:, p * LANES : (p + 1) * LANES] = turn(part, cos_ref[...], -sin_ref[...]).astype(bf16)


def after_keys_kernel(
    dkv0, dkv1, dkv2, dkv3, dq_ref, x_ref, w_ref, cos_ref, sin_ref, g_ref, y_ref, gain_ref
):
    whole = dkv0[...].astype(f32) + dkv1[...].astype(f32)
    whole = whole + (dkv2[...].astype(f32) + dkv3[...].astype(f32))
    g_ref[:, : 3 * LANES] = dq_ref[...]
    g_ref[:, 3 * LANES : 4 * LANES] = turn(whole[:, :LANES], cos_ref[...], -sin_ref[...]).astype(bf16)
    g_ref[:, 4 * LANES :] = whole[:, LANES:].astype(bf16)
    y = nt(g_ref[...], w_ref[...])
    y_ref[...] = y.astype(bf16)
    x = x_ref[...].astype(f32)
    root = lax.rsqrt(jnp.mean(x * x, axis=-1, keepdims=True) + epsilon)
    gain_ref[...] = jnp.broadcast_to(jnp.sum(y * (x * root), axis=0, keepdims=True), gain_ref.shape)


CHUNK = 256
HALF = CHUNK // GROUP * SLOTS


def picks(tgt_ref, ch):
    at = slice(ch * CHUNK, (ch + 1) * CHUNK)
    rows = iota((HALF, CHUNK), 0)
    return rows == tgt_ref[0:1, at], rows == tgt_ref[1:2, at]


def one_hot(pick_a, pick_b):
    return jnp.concatenate([pick_a.astype(f32), pick_b.astype(f32)], axis=0).astype(bf16)


def row_of(table, expert):
    return jnp.sum(jnp.where(iota(table.shape, 0) == expert, table, 0.0), axis=0, keepdims=True)


def two_of(refs, ch):
    return jnp.concatenate([refs[2 * ch][...], refs[2 * ch + 1][...]], axis=0)


def put_two(refs, ch, value):
    rows = value.shape[0] // 2
    refs[2 * ch][...] = value[:rows]
    refs[2 * ch + 1][...] = value[rows:]


def experts_kernel(s_ref, router, wg, wu, wd, *refs):
    tokens_in, refs = refs[: 2 * SIDE], refs[2 * SIDE :]
    tgt, mask, *refs = refs
    tokens_out, refs = refs[: 2 * SIDE], refs[2 * SIDE :]
    gates, slots_in, g_ref, u_ref, hidden, weights, scaled = refs
    chunks = SIDE
    for ch in range(chunks):
        at = slice(ch * CHUNK, (ch + 1) * CHUNK)
        z = nt(router[...], two_of(tokens_in, ch))
        chosen = mask[:, at]
        z = jnp.where(chosen > 0.0, z, -1e30)
        e = jnp.exp(z - jnp.max(z, axis=0, keepdims=True)) * chosen
        gates[:, at] = e / jnp.sum(e, axis=0, keepdims=True)
    rows = slots_in.shape[0] // 2
    for ch in range(chunks):
        pick_a, pick_b = picks(tgt, ch)
        got = nn(one_hot(pick_a, pick_b), two_of(tokens_in, ch)).astype(bf16)
        here = gates[:, ch * CHUNK : (ch + 1) * CHUNK]
        for which, pick in enumerate((pick_a, pick_b)):
            at = which * rows + ch * HALF
            slots_in[at : at + HALF, :] = got[which * HALF : (which + 1) * HALF]
            weight = jnp.sum(jnp.where(pick, row_of(here, s_ref[which]), 0.0), axis=1, keepdims=True)
            weights[at : at + HALF, :] = jnp.broadcast_to(weight, (HALF, LANES))
    hidden[...] = jnp.zeros_like(hidden)
    for k in range(wg.shape[1] // BLOCK):
        at = slice(k * BLOCK, (k + 1) * BLOCK)
        here = pl.ds(pl.multiple_of(s_ref[2 + k] * rows, rows), rows)
        both = nn(slots_in[here, :], jnp.concatenate([wg[:, at], wu[:, at]], axis=1))
        g, u = both[:, :BLOCK], both[:, BLOCK:]
        g_ref[:, at] = g
        u_ref[:, at] = u
        hidden[here, at] = (g * jax.nn.sigmoid(g) * u).astype(bf16)
    for at in range(0, wd.shape[1], CHUNK):
        part = nn(hidden[...], wd[:, at : at + CHUNK])
        scaled[:, at : at + CHUNK] = (part * weights[:, 0:1]).astype(bf16)
    for ch in range(chunks):
        at = ch * HALF
        both = jnp.concatenate([scaled[at : at + HALF], scaled[rows + at : rows + at + HALF]], axis=0)
        put_two(tokens_out, ch, tn(one_hot(*picks(tgt, ch)), both).astype(bf16))


def experts_back_kernel(s_ref, router, wg, wu, wd, *refs):
    grads_in, refs = refs[: 2 * SIDE], refs[2 * SIDE :]
    tgt, gates, g_ref, u_ref, *refs = refs
    grads_out, refs = refs[: 2 * SIDE], refs[2 * SIDE :]
    dgu_ref, h_ref, dy, dz_ref, inner, back = refs
    chunks = SIDE
    rows = dy.shape[0] // 2
    for ch in range(chunks):
        pick_a, pick_b = picks(tgt, ch)
        here = gates[:, ch * CHUNK : (ch + 1) * CHUNK]
        got = nn(one_hot(pick_a, pick_b), two_of(grads_in, ch))
        for which, pick in enumerate((pick_a, pick_b)):
            weight = jnp.sum(jnp.where(pick, row_of(here, s_ref[which]), 0.0), axis=1, keepdims=True)
            at = which * rows + ch * HALF
            dy[at : at + HALF, :] = (got[which * HALF : (which + 1) * HALF] * weight).astype(bf16)
    inner[...] = jnp.zeros_like(inner)
    back[...] = jnp.zeros_like(back)
    for k in range(wg.shape[1] // BLOCK):
        at = slice(k * BLOCK, (k + 1) * BLOCK)
        here = pl.ds(pl.multiple_of(s_ref[2 + k] * rows, rows), rows)
        dh = nt(dy[here, :], wd[at, :])
        g, u = g_ref[:, at], u_ref[:, at]
        sig = jax.nn.sigmoid(g)
        swish = g * sig
        h = (swish * u).astype(bf16)
        h_ref[:, at] = h
        inner[here, :] += jnp.broadcast_to(
            jnp.sum(h.astype(f32) * dh, axis=1, keepdims=True), (rows, LANES)
        )
        dg = (dh * u * sig * (1.0 + g * (1.0 - sig))).astype(bf16)
        du = (dh * swish).astype(bf16)
        both = jnp.concatenate([dg, du], axis=1)
        dgu_ref[:, 2 * k * BLOCK : 2 * (k + 1) * BLOCK] = both
        back[here, :] += nt(both, jnp.concatenate([wg[:, at], wu[:, at]], axis=1))
    for ch in range(chunks):
        pick_a, pick_b = picks(tgt, ch)
        span = slice(ch * CHUNK, (ch + 1) * CHUNK)
        sums = []
        for which, pick in enumerate((pick_a, pick_b)):
            at = which * rows + ch * HALF
            column = inner[at : at + HALF, 0:1]
            sums.append(jnp.sum(jnp.where(pick, column, 0.0), axis=0, keepdims=True))
        table = gates[:, span]
        expert = iota(table.shape, 0)
        dz = jnp.where(expert == s_ref[0], sums[0], 0.0) + jnp.where(expert == s_ref[1], sums[1], 0.0)
        dz = dz - table * (sums[0] + sums[1])
        high = dz.astype(bf16)
        lower = (dz - high.astype(f32)).astype(bf16)
        dz_ref[:, span] = jnp.concatenate([high, lower], axis=0)
        at = ch * HALF
        moved = jnp.concatenate([back[at : at + HALF, :], back[rows + at : rows + at + HALF, :]], axis=0)
        value = tn(
            jnp.concatenate([one_hot(pick_a, pick_b), high], axis=0),
            jnp.concatenate([moved.astype(bf16), router[...]], axis=0),
        )
        put_two(grads_out, ch, value.astype(bf16))


def router_kernel(dz_ref, *refs):
    tokens_in, (router_grad,) = refs[: 2 * SIDE], refs[2 * SIDE :]
    total = 0.0
    for ch in range(SIDE):
        total = total + nn(dz_ref[:, ch * CHUNK : (ch + 1) * CHUNK], two_of(tokens_in, ch))
    rows = router_grad.shape[0]
    total = total[:rows] + total[rows:]
    router_grad[...] = total + jnp.where(pl.program_id(0) == 0, 0.0, router_grad[...])


def expert_weights_kernel(
    s_ref, b_own, o0, o1, o2, h, dy, dgu, gate, up, near, far, down
):
    rows, size = h.shape[0], o1.shape[0]
    half = s_ref[2 + h.shape[1] // BLOCK]
    begin = pl.program_id(0) == 0
    for k in range(h.shape[1] // BLOCK):
        at = slice(k * BLOCK, (k + 1) * BLOCK)
        wide = slice(2 * k * BLOCK, 2 * (k + 1) * BLOCK)
        here = pl.ds(pl.multiple_of(s_ref[2 + k] * rows, rows), rows)
        first = s_ref[2 + k] == 0
        theirs = [jnp.where(first, o0[:size], o1[...]), jnp.where(first, o0[size:], o2[...])]
        both = tn(
            jnp.concatenate([b_own[here, :], *theirs], axis=0),
            jnp.concatenate([dgu[half, :, wide], dgu[1 - half, :, wide]], axis=0),
        )
        low = tn(h[:, at], dy[here, :])
        gate[:, at] = both[:, :BLOCK] + jnp.where(begin, 0.0, gate[:, at])
        up[:, at] = both[:, BLOCK:] + jnp.where(begin, 0.0, up[:, at])
        low = low + jnp.where(begin, 0.0, down[at, :])
        down[at, :] = low
        cut = at.start - near.shape[0]
        if cut < 0:
            near[at, :] = low.astype(bf16)
        else:
            far[cut : cut + BLOCK, :] = low.astype(bf16)


def ring(stage, steps):
    pairs = []
    for x in range(SIDE):
        for z in range(SIDE):
            for core in range(2):
                along_x = (core == 0) == (stage == 0)
                to = ((x + steps) % SIDE, z) if along_x else (x, (z + steps) % SIDE)
                pairs.append(((x * SIDE + z) * 2 + core, (to[0] * SIDE + to[1]) * 2 + core))
    return pairs


def other_core(value):
    return lax.ppermute(value, "ep", [(i, i ^ 1) for i in range(2 * CHIPS)])


def other_half(value):
    return lax.ppermute(value, "tp", [(0, 1), (1, 0)])


def other_both(value):
    pairs = [(2 * i + t, 2 * (i ^ 1) + 1 - t) for i in range(2 * CHIPS) for t in range(2)]
    return lax.ppermute(value, ("ep", "tp"), pairs)


def in_order(own, other, place, dim):
    return jnp.concatenate(
        [jnp.where(place == 0, own, other), jnp.where(place == 0, other, own)], axis=dim
    )


def from_ring(value, stage):
    return [value] + [lax.ppermute(value, "ep", ring(stage, -d)) for d in range(1, SIDE)]


def to_ring(pieces, stage):
    return [pieces[0]] + [
        lax.ppermute(pieces[d], "ep", ring(stage, d)) for d in range(1, SIDE)
    ]


def everyone(value):
    return from_ring(jnp.concatenate(from_ring(value, 0), axis=1), 1)


def added(pieces):
    pieces = [p.astype(f32) for p in pieces]
    return (pieces[0] + pieces[1]) + (pieces[2] + pieces[3])


def pieces_of(value):
    size = value.shape[1] // SIDE
    return [value[:, d * size : (d + 1) * size] for d in range(SIDE)]


def to_owners(pieces, beside=()):
    joined, *beside = pin(added(to_ring(pieces, 1)).astype(bf16), *beside)
    return to_ring(pieces_of(joined), 0), beside


def pin(*values):
    return lax.optimization_barrier(values)


SAME_CORE = [[2 * chip + core for chip in range(CHIPS)] for core in range(2)]


def exchange(pieces, groups=SAME_CORE):
    return lax.all_to_all(pieces, "ep", 0, 0, tiled=True, axis_index_groups=groups)


def broadcast(value, count=CHIPS, groups=SAME_CORE):
    return exchange(jnp.broadcast_to(value[None], (count, *value.shape)), groups)


def half_of(value, place, dim=0):
    size = value.shape[dim] // 2
    mine = lax.dynamic_slice_in_dim(value, place * size, size, dim)
    rest = lax.dynamic_slice_in_dim(value, (1 - place) * size, size, dim)
    return mine, rest


def body(
    x_in, cotangent, norm1_gain, wq, wk, wv, wo, norm2_gain, router, w_gate, w_up, w_down, routes
):
    section = lax.axis_index("section")
    rank = lax.axis_index("ep")
    half = lax.axis_index("tp")
    chip, core = rank // 2, rank % 2
    x, z = chip // SIDE, chip % SIDE
    micros, core_rows, width = x_in.shape
    own_rows = core_rows // 2
    chip_rows = core_rows * 2
    length = chip_rows * CHIPS
    experts = router.shape[2]
    blocks = w_gate.shape[2] // BLOCK
    gain_one = norm1_gain.reshape(1, width)
    gain_two = norm2_gain.reshape(1, width)
    gate_w, up_w, down_w = w_gate[0], w_up[0], w_down[0]
    expert_rows = -(-experts // 16) * 16
    router_t = jnp.pad(router[0].T, ((0, expert_rows - experts), (0, 0)))

    qkv_w = jnp.concatenate([half_of(w[0], core, 1)[0] for w in (wq, wk, wv)], axis=1)
    out_w = half_of(wo[0], core)[0]

    first_row = (chip * chip_rows).astype(jnp.int32)
    positions = (first_row + jnp.arange(chip_rows, dtype=jnp.int32)).astype(f32)
    quarter = HEAD // 2
    frequency = 10000.0 ** (-jnp.arange(quarter, dtype=f32) * 2.0 / HEAD)
    phase = positions[:, None] * frequency[None, :]
    cosine = jnp.tile(jnp.cos(phase), (1, 4))
    sine = jnp.concatenate([-jnp.sin(phase), jnp.sin(phase)] * 2, axis=1)

    def chips_met(which_core):
        inner, outer = jnp.arange(CHIPS) % SIDE, jnp.arange(CHIPS) // SIDE
        by_x = jnp.where(which_core == 0, inner, outer)
        by_z = jnp.where(which_core == 0, outer, inner)
        return ((x + by_x) % SIDE) * SIDE + (z + by_z) % SIDE

    row_scalars = jnp.concatenate(
        [first_row.reshape(1), chips_met(core) * chip_rows]
    ).astype(jnp.int32)

    first_expert = rank * blocks // EXPERT_BLOCKS
    which = (rank * blocks + jnp.arange(blocks)) // EXPERT_BLOCKS - first_expert
    scalars = jnp.concatenate(
        [jnp.stack([first_expert, first_expert + 1]), which, half.reshape(1)]
    ).astype(jnp.int32)

    tokens = CHIPS * own_rows
    slot_rows = 2 * 2 * CHIPS * SLOTS
    hidden_width = blocks * BLOCK
    both_rows = micros * chip_rows
    cosines, sines = jnp.tile(cosine, (micros, 1)), jnp.tile(sine, (micros, 1))

    def prepare(own_routes):
        all_routes = broadcast(own_routes.reshape(-1, LANES), 2 * CHIPS, None)
        met = jnp.concatenate([chips_met(core) * 2 + core, chips_met(1 - core) * 2 + 1 - core])
        all_routes = jnp.take(all_routes, met, axis=0)
        both_routes = all_routes.reshape(2 * CHIPS, micros, own_rows, TOPK).transpose(1, 0, 2, 3)
        both_routes = both_routes.reshape(micros, 2 * CHIPS * own_rows, TOPK)
        named = (
            both_routes[:, None, :, :] == jnp.arange(expert_rows, dtype=jnp.int32)[None, :, None, None]
        )
        masks = jnp.any(named, axis=-1).astype(f32)
        wanted = jnp.stack([first_expert, first_expert + 1]).astype(jnp.int32)
        hits = jnp.any(both_routes[:, None, :, :] == wanted[None, :, None, None], axis=-1)
        hits = hits.reshape(micros, 2, 2 * CHIPS, own_rows).astype(jnp.int32)
        before = jnp.cumsum(hits, axis=-1) - hits
        base = (jnp.arange(2 * CHIPS, dtype=jnp.int32) % (CHUNK // GROUP)) * SLOTS
        targets = jnp.where(hits > 0, base[None, None, :, None] + before, -1)
        targets = targets.reshape(micros, 2, 2 * CHIPS * own_rows)
        return targets, masks

    def project(x128):
        a, q, kv = local_call(
            project_kernel,
            [((both_rows, width), bf16), ((both_rows, 3 * LANES), bf16), ((both_rows, 2 * LANES), bf16)],
            [x128.reshape(both_rows, width), gain_one, qkv_w, cosines, sines],
            flops=2 * both_rows * width * 5 * LANES,
            vmem=16,
        )
        return a, q.reshape(micros, chip_rows, -1), kv.reshape(micros, chip_rows, -1)

    def attend(q, kv):
        return local_call(
            attend_kernel,
            [((chip_rows, 3 * LANES), bf16), ((8, 6 * chip_rows), f32), ((chip_rows, width), bf16)],
            [row_scalars, out_w],
            each=[q, *kv],
            scratch=[((6 * chip_rows, LANES), bf16), ((length, 6 * chip_rows), f32)],
            flops=8 * micros * length * 6 * chip_rows * LANES,
            smem=1,
            vmem=32,
            micros=micros,
        )

    def attend_back(q, kv, grad, log_total, o):
        return local_call(
            attend_back_kernel,
            [((chip_rows, 3 * LANES), bf16)] + [((length // SIDE, 2 * LANES), bf16)] * SIDE,
            [row_scalars, out_w, cosine, sine],
            each=[q, *kv, grad, log_total, o],
            scratch=[
                ((6 * chip_rows, LANES), bf16),
                ((6 * chip_rows, LANES), bf16),
                ((chip_rows, 3 * LANES), bf16),
                ((6 * chip_rows, LANES), f32),
            ],
            flops=20 * micros * length * 6 * chip_rows * LANES,
            smem=1,
            vmem=60,
            micros=micros,
        )

    def after_keys(arrived, dq, x128):
        dqkv, y, gain = local_call(
            after_keys_kernel,
            [((both_rows, 5 * LANES), bf16), ((both_rows, width), bf16), ((8, width), f32)],
            [v.reshape(both_rows, -1) for v in (*arrived, dq, x128)] + [qkv_w, cosines, sines],
            flops=2 * both_rows * width * 5 * LANES,
            vmem=16,
        )
        return dqkv, y.reshape(micros, chip_rows, width), gain[:1]

    piece = ((tokens // SIDE, width), bf16)

    def run_experts(arrived):
        result = local_call(
            experts_kernel,
            [piece] * (2 * SIDE)
            + [
                ((expert_rows, 2 * tokens), f32),
                ((slot_rows, width), bf16),
                ((slot_rows // 2, hidden_width), f32),
                ((slot_rows // 2, hidden_width), f32),
            ],
            [scalars, router_t, gate_w, up_w, down_w],
            each=[*arrived, targets, masks],
            scratch=[
                ((slot_rows, hidden_width), bf16),
                ((slot_rows, LANES), f32),
                ((slot_rows, width), bf16),
            ],
            flops=10 * micros * slot_rows * hidden_width * width,
            smem=1,
            vmem=48,
            micros=micros,
        )
        return result[: 2 * SIDE], result[2 * SIDE :]

    def run_experts_back(grads, gates, g, u):
        result = local_call(
            experts_back_kernel,
            [piece] * (2 * SIDE)
            + [
                ((slot_rows // 2, 2 * hidden_width), bf16),
                ((slot_rows // 2, hidden_width), bf16),
                ((slot_rows, width), bf16),
                ((2 * expert_rows, 2 * tokens), bf16),
            ],
            [scalars, router_t, gate_w, up_w, down_w],
            each=[*grads, targets, gates, g, u],
            scratch=[((slot_rows, LANES), f32), ((slot_rows, width), f32)],
            flops=10 * micros * slot_rows * hidden_width * width,
            smem=1,
            vmem=52,
            micros=micros,
        )
        return result[: 2 * SIDE], result[2 * SIDE :]

    def sum_four(part):
        mine, rest = half_of(part, core, 1)
        mine, rest = half_of(mine.astype(f32) + other_core(rest).astype(f32), half, 1)
        return mine + other_half(rest.astype(bf16)).astype(f32)

    def to_four(rows32):
        rows64 = in_order(rows32, other_half(rows32), half, 1)
        return in_order(rows64, other_core(rows64), core, 1)

    def over_cores(parts):
        return [
            (own.astype(f32) + other_core(other).astype(f32)).astype(bf16)
            for own, other in zip(parts[:SIDE], parts[SIDE:])
        ]

    def tokens_back(parts, beside=()):
        pieces, beside = to_owners(over_cores(parts), beside)
        return added(pieces), beside

    def inverse_root(values):
        return lax.rsqrt(jnp.mean(values * values, axis=-1, keepdims=True) + epsilon)

    def norm_back(values, root, gradient, gain):
        weighted = gradient * gain
        return root * weighted - values * root**3 * jnp.mean(weighted * values, axis=-1, keepdims=True)

    def forward(own, x128, sent=None):
        nonlocal targets, masks
        a, q, kv = project(x128)
        kv_all = everyone(kv)
        o, log_total, y = attend(q, kv_all)
        residual = own.astype(f32) + sum_four(y)
        mixed = (residual * inverse_root(residual) * gain_two).astype(bf16)
        if sent is not None:
            own_routes = lax.dynamic_slice_in_dim(routes[0], half * own_rows, own_rows, 1)
            targets, masks = prepare(pin(own_routes, kv_all[0])[0])
            mixed = jnp.where(section == 0, mixed, sent)
        arrived = everyone(mixed)
        if sent is not None:
            *arrived, targets, masks = pin(*arrived, targets, masks)
        arrived = arrived + [other_core(p) for p in arrived]
        parts, rest = run_experts(arrived)
        return parts, (own, x128, a, q, kv_all, o, log_total, residual, arrived, *rest)

    def backward(grad_rows, grads, kept, between=None):
        residual, _, gates, _, g, u = kept[7:]
        parts, rest = run_experts_back(grads, gates, g, u)
        if between is None:
            mixed_grad = tokens_back(parts)[0]
        else:
            parts = between(*between(*parts, finish=True), start=True)
            (router_grad,) = local_call(
                router_kernel,
                [],
                [],
                each=[rest[3], *kept[8]],
                sums=[((expert_rows, width), f32)],
                flops=4 * micros * expert_rows * 2 * tokens * width,
                vmem=20,
                micros=micros,
            )
            pieces = to_ring(over_cores(parts), 1)
            joined, router_grad = between(added(pieces).astype(bf16), router_grad, finish=True)
            rest = (*rest[:3], router_grad)
            mixed_grad = added(to_ring(pieces_of(joined), 0))
        root = inverse_root(residual)
        gain_two_grad = jnp.sum(mixed_grad * residual * root, axis=(0, 1))
        resid_grad = grad_rows.astype(f32) + norm_back(residual, root, mixed_grad, gain_two)
        return resid_grad, rest, gain_two_grad

    targets = masks = None
    own_x = lax.dynamic_slice_in_dim(x_in, half * own_rows, own_rows, 1)
    x128 = in_order(x_in, other_core(x_in), core, 1)
    parts, kept = forward(own_x, x128, cotangent)
    upper_grads = kept[8]
    out = (kept[7] + tokens_back(parts)[0]).astype(bf16)
    same = lax.ppermute(out, "section", [(0, 1)])
    rows64 = in_order(same, lax.ppermute(out, ("section", "tp"), [(0, 3), (1, 2)]), half, 1)
    whole = in_order(rows64, other_core(rows64), core, 1)
    last_parts, kept = forward(
        jnp.where(section == 0, own_x, same), jnp.where(section == 0, x128, whole)
    )
    own, x128, a, q, kv_all, o, log_total, residual = kept[:8]
    own, slots_in = own.astype(f32), kept[10]

    resid_grad, *_ = backward(cotangent, upper_grads, kept)
    low, *joined = pin(resid_grad.astype(bf16), *over_cores(last_parts))
    pieces = to_ring(joined, 1)
    out_grad, rows = pin(to_four(low), slots_in[:, : slot_rows // 2])
    other_slots = [other_half(rows)]
    dq, *dkv = attend_back(q, kv_all, out_grad, log_total, o)
    *dkv, joined = pin(*dkv, added(pieces).astype(bf16))
    dkv, _ = to_owners(dkv)
    *dkv, joined, other_slots[0] = pin(*dkv, joined, other_slots[0])
    pieces = to_ring(pieces_of(joined), 0)
    _, y, _ = after_keys(dkv, dq, x128)
    normed_grad, out = pin(sum_four(y), (residual + added(pieces)).astype(bf16))
    root = inverse_root(own)
    upper = (resid_grad + norm_back(own, root, normed_grad, gain_one)).astype(bf16)
    coming = lax.ppermute(upper, "section", [(1, 0)])
    coming, other_out = pin(jnp.where(section == 0, coming, cotangent), other_half(out))
    activations = in_order(out, other_out, half, 1)

    cuts = [0, slot_rows // 2, slot_rows * 3 // 4, slot_rows]

    def between(*values, finish=False, start=False):
        if finish:
            *values, other_slots[-1] = pin(*values, other_slots[-1])
        if start:
            at, end = cuts[len(other_slots) :][:2]
            *values, rows = pin(*values, slots_in[:, at:end])
            other_slots.append(other_half(rows))
        return values

    arrived = between(*everyone(coming), start=True)
    grads = arrived + [other_core(p) for p in arrived]
    resid_grad, (dgu, h, dy, router_grad), gain_two_grad = backward(coming, grads, kept, between)
    out_grad = to_four(resid_grad.astype(bf16))
    all_dgu = lax.all_gather(dgu, "tp")
    out_w_grad = tn(o.reshape(both_rows, -1), out_grad.reshape(both_rows, width)).astype(bf16)
    out_w_grad = exchange(out_w_grad.reshape(CHIPS, -1, width))
    dq, *dkv = attend_back(q, kv_all, out_grad, log_total, o)
    dq, out_w_grad = pin(dq, out_w_grad)
    out_w_grad = jnp.sum(out_w_grad.astype(f32), axis=0).astype(bf16)
    near_rows = 2 * BLOCK
    gate_grad, up_grad, near, far = local_call(
        expert_weights_kernel,
        [],
        [scalars],
        each=[slots_in, *other_slots, h, dy],
        pairs=[all_dgu],
        sums=[
            ((width, hidden_width), f32),
            ((width, hidden_width), f32),
            ((near_rows, width), bf16),
            ((hidden_width - near_rows, width), bf16),
        ],
        scratch=[((hidden_width, width), f32)],
        flops=10 * slot_rows * hidden_width * width,
        smem=1,
        vmem=56,
        micros=micros,
    )
    all_out = lax.all_gather(out_w_grad, "ep")
    q_grad = tn(a, dq.reshape(both_rows, -1)).astype(bf16)
    q_grad = exchange(q_grad.reshape(CHIPS, -1, 3 * LANES))
    near_down = other_half(near)
    arrived, (gate_grad, up_grad, q_grad) = to_owners(dkv, (gate_grad, up_grad, q_grad))
    *arrived, near_down = pin(*arrived, near_down)
    q_grad = jnp.sum(q_grad.astype(f32), axis=0).astype(bf16)
    dqkv, y, gain_one_grad = after_keys(arrived, dq, x128)

    kv_width = 2 * LANES
    small = jnp.concatenate([router_grad[:experts], gain_one_grad, gain_two_grad[None]], axis=0)
    small_count = small.size
    small_lines = -(-small_count // (CHIPS * kv_width))
    small = jnp.pad(small.reshape(-1), (0, CHIPS * small_lines * kv_width - small_count))
    small = small.reshape(CHIPS, small_lines, kv_width).astype(bf16)
    wide = tn(a, dqkv[:, 3 * LANES :]).astype(bf16).reshape(CHIPS, -1, kv_width)
    lines = wide.shape[1]
    wide, all_out = pin(jnp.concatenate([wide, small], axis=1), all_out)
    all_q = lax.all_gather(pin(q_grad, all_out)[0], "ep")
    far_down = other_half(pin(far, near_down)[0])
    wide, y, far_down = pin(exchange(wide), y, far_down)
    normed_grad = sum_four(y)
    wide, normed_grad, all_q = pin(
        broadcast(jnp.sum(wide.astype(f32), axis=0).astype(bf16)), normed_grad, all_q
    )
    input_grads = (resid_grad + norm_back(own, root, normed_grad, gain_one)).astype(bf16)
    down_grad = jnp.concatenate(
        [near.astype(f32) + near_down.astype(f32), far.astype(f32) + far_down.astype(f32)], axis=0
    )
    small = wide[:, lines:].reshape(-1)[:small_count].reshape(experts + 2, width)
    small = small.astype(f32) + other_core(small).astype(f32)
    small = small + other_half(small.astype(bf16)).astype(f32)
    wide = wide[:, :lines].reshape(width, kv_width)
    other_wide = other_core(wide)

    def both_cores(start, end):
        return in_order(wide[:, start:end], other_wide[:, start:end], core, 1).astype(f32)

    grad_k = both_cores(0, LANES)
    grad_v = both_cores(LANES, 2 * LANES)
    all_q = all_q.reshape(CHIPS, 2, -1, 3 * LANES)
    grad_q = jnp.concatenate(
        [all_q[:, c].reshape(width, -1) for c in range(2)], axis=1
    ).astype(f32)
    all_out = all_out.reshape(CHIPS, 2, -1, width)
    grad_out = jnp.concatenate(
        [all_out[:, c].reshape(-1, width) for c in range(2)], axis=0
    ).astype(f32)
    return (
        activations[None],
        input_grads[None],
        small[experts][None],
        grad_q[None],
        grad_k[None],
        grad_v[None],
        grad_out[None],
        small[experts + 1][None],
        small[:experts].T[None],
        gate_grad[None],
        up_grad[None],
        down_grad[None],
    )


def solution(mesh):
    ep = "ep"
    ep_tp = ("ep", "tp")
    placed = (
        P(None, ep, None),
        P(None, ep_tp, None),
        P("section", None),
        P("section", None, "tp"),
        P("section", None, "tp"),
        P("section", None, "tp"),
        P("section", "tp", None),
        P("section", None),
        P("section", None, None),
        P("section", None, ep),
        P("section", None, ep),
        P("section", ep, None),
        P("section", None, ep, None),
    )
    return jax.shard_map(
        body,
        mesh=mesh,
        in_specs=placed,
        out_specs=(
            P("section", None, ep, None),
            P("section", None, ep_tp, None),
            P("section", None),
            P("section", None, "tp"),
            P("section", None, "tp"),
            P("section", None, "tp"),
            P("section", "tp", None),
            P("section", None),
            P("section", None, None),
            P("section", None, ep),
            P("section", None, ep),
            P("section", ep, None),
        ),
        check_vma=False,
    )
```
